512 devices in a mesh: pair: 16 (over z, core), virt: 32 (over x, y).
Axes of the slice: x: 4, y: 8, z: 8, core: 2. Of those that a mesh axis runs over, the one named last changes fastest.
Arguments:
- lam: bfloat16 [16, 16, 256, 256], P('pair', None, 'virt'), may hold values from -4 to 4
- drive: float32 [16, 16, 256, 256], P('pair', None, 'virt'), may hold values from -45 to 45
- order: int32 [16, 16], P('pair'), may hold values from 0 to 15, each once within a row
- dom_tiles: int32 [16, 16, 2], P('pair'), may hold values from 0 to 31, as said below
- dom_len: int32 [16, 16], P('pair'), may hold values from 1 to 2, as said below
- factors: bfloat16 [32, 4, 128, 128], P('virt'), may hold values from -0.5 to 0.5
- e_occ: float32 [16], replicated, may hold values from -1.2 to -0.4
- e_virt: bfloat16 [32, 128], P('virt'), may hold values from 0.19921875 to 3
Outputs:
- lam_next: bfloat16 [16, 16, 256, 256], P('pair', None, 'virt')
- res_norm: float32 [2, 16, 16], P(None, 'pair')
The draws below stay inside these ranges and needn't reach their ends.
Inputs may be any that keep to these rules, and one draw needn't show every extreme that they name: Each row is a permutation; order[i, s] = j puts the pair (i, j) in slot s of row i. dom_tiles[i, j] = dom_tiles[j, i]; the tiles of one pair are distinct. dom_len[i, j] = dom_len[j, i]; every pair (i, i) has all 2 tiles live.
All inputs are finite; a program needn't handle non-finite values.
Results may differ from the reference program's by a relative error of at most 0.0054.
Values may be sent and summed in bfloat16 or wider, within the bound.
A program may use at most 64 MiB of HBM per device.

```python
import math
from functools import partial
import jax
import jax.numpy as jnp
from jax import lax

TILE = 128
NQ = 4
DOM_T = 2
ITERS = 2
NOCC = 16
NT = 32
DM = 256


def draw_drive(key, part):
    key = jax.random.fold_in(key, 13)
    first, second, third = jax.random.split(key, 3)
    shape = (NOCC, NOCC, DM, DM)
    noise = jnp.clip(jax.random.normal(first, shape, jnp.float32), -5.0, 5.0)
    position = jnp.arange(DM, dtype=jnp.float32) / DM
    row_scale = jnp.exp(math.log(3.0) * position) * jnp.exp(math.log(3.0) * jax.random.uniform(second, (NOCC, NOCC, DM), jnp.float32))
    col_scale = jnp.exp(math.log(3.3) * jax.random.uniform(third, (NOCC, NOCC, DM), jnp.float32))
    return 0.3 * noise * row_scale[:, :, :, None] * col_scale[:, :, None, :]


def draw_factors(key, part):
    key = jax.random.fold_in(key, 14)
    first, second = jax.random.split(key, 2)
    shape = (NT, NQ, TILE, TILE)
    noise = jnp.clip(jax.random.normal(first, shape, jnp.float32), -4.0, 4.0)
    block_count = max(TILE // 8, 1)
    levels = jnp.exp(jax.random.uniform(second, (NT, block_count), jnp.float32, -1.2, 1.2))
    row_block = jnp.minimum(jnp.arange(TILE, dtype=jnp.int32) // 8, block_count - 1)
    row_level = jnp.take(levels, row_block, axis=1)
    scale = 1.0 / math.sqrt(TILE * NQ)
    values = noise * scale * row_level[:, None, :, None]
    return jnp.clip(values, -0.5, 0.5).astype(jnp.bfloat16)


def draw_dom_tiles(key, part):
    key = jax.random.fold_in(key, 11)
    first, second = jax.random.split(key, 2)
    starts = jax.random.randint(first, (NOCC, NOCC), 0, NT)
    upper = jnp.arange(NOCC)[:, None] <= jnp.arange(NOCC)[None, :]
    starts = jnp.where(upper, starts, starts.T)
    starts = starts.at[0, 0].set(NT - 1)
    span = (NT - 1) // max(DOM_T - 1, 1)
    gaps = jax.random.randint(second, (NOCC, NOCC, max(DOM_T - 1, 1)), 1, span + 1)
    gaps = jnp.where(upper[:, :, None], gaps, jnp.transpose(gaps, (1, 0, 2)))
    gaps = gaps[:, :, :DOM_T - 1]
    offsets = jnp.concatenate([jnp.zeros((NOCC, NOCC, 1), jnp.int32), jnp.cumsum(gaps, axis=2).astype(jnp.int32)], axis=2)
    return ((starts[:, :, None] + offsets) % NT).astype(jnp.int32)


def draw_dom_len(key, part):
    key = jax.random.fold_in(key, 12)
    lengths = jax.random.randint(key, (NOCC, NOCC), 1, DOM_T + 1)
    upper = jnp.arange(NOCC)[:, None] <= jnp.arange(NOCC)[None, :]
    lengths = jnp.where(upper, lengths, lengths.T)
    diagonal = jnp.arange(NOCC)[:, None] == jnp.arange(NOCC)[None, :]
    return jnp.where(diagonal, DOM_T, lengths).astype(jnp.int32)


def block_scale(stream_key, dims, pieces, smallest, largest):
    factor_of, own = 1.0, jax.random.fold_in(stream_key, 6)
    for dim, parts in pieces:
        heights = jnp.exp(jax.random.uniform(jax.random.fold_in(own, dim), (parts,), jnp.float32, smallest / len(pieces), largest / len(pieces)))
        factor_of = factor_of * jnp.repeat(heights, dims[dim] // parts).reshape([-1 if axis == dim else 1 for axis in range(len(dims))])
    return factor_of


def centred(rng, dims, scale, most, shards=(), kind=jnp.bfloat16):
    gain = block_scale(rng, dims, shards, -0.22, 0.18) if shards else 1.0
    entries = jax.random.normal(rng, dims, jnp.float32) * scale * gain
    return jnp.minimum(jnp.maximum(entries, -most), most).astype(kind)


def setup_inputs(seed: int = 0) -> dict:
    key_of = jax.random.split(jax.random.key(seed), 9)
    return {
        "lam": centred(key_of[0], (NOCC, NOCC, DM, DM), 0.5, 4.0, ((0, 16), (2, 32))),
        "drive": draw_drive(jax.random.fold_in(key_of[8], 71), 0),
        "order": jax.vmap(lambda own: jax.random.permutation(own, NOCC))(jax.random.split(key_of[2], NOCC)).reshape((NOCC, NOCC)).astype(jnp.int32),
        "dom_tiles": draw_dom_tiles(jax.random.fold_in(key_of[8], 71), 0),
        "dom_len": draw_dom_len(jax.random.fold_in(key_of[8], 71), 0),
        "factors": draw_factors(jax.random.fold_in(key_of[8], 71), 0),
        "e_occ": jnp.clip(jax.random.uniform(key_of[6], (NOCC,), jnp.float32, -1.2, -0.4), -1.2, -0.4),
        "e_virt": jnp.clip(jnp.exp(math.log(3.0) - 2.7119641 * jax.random.uniform(key_of[7], (NT, TILE), jnp.float32) ** block_scale(key_of[7], (NT, TILE), ((0, 32),), -0.2, 0.2)), 0.19921875, 3.0).astype(jnp.bfloat16),
    }


def flatten_pairs(values):
    return values.reshape((values.shape[0] * values.shape[1],) + values.shape[2:])

def pair_update(items, factors, e_virt):
    summed, own, source, tile_ids, length, occ_pair = items
    dom_width = DOM_T * TILE
    pair_factors = jnp.take(factors, tile_ids, axis=0).astype(jnp.float32)
    block_four = summed.astype(jnp.float32).reshape(DOM_T, TILE, DOM_T, TILE)
    half_prod = jnp.einsum('kald,lqbd->qkalb', block_four, pair_factors).astype(jnp.bfloat16)
    half_prod = lax.optimization_barrier(half_prod)
    ladder = jnp.einsum('kqac,qkclb->kalb', pair_factors, half_prod.astype(jnp.float32))
    ladder = lax.optimization_barrier(ladder.reshape(dom_width, dom_width).astype(jnp.bfloat16))
    ladder = ladder.astype(jnp.float32)
    energy = jnp.take(e_virt, tile_ids, axis=0).astype(jnp.float32).reshape(dom_width)
    denominator = energy[:, None] + energy[None, :] - occ_pair
    live_pos = jnp.arange(dom_width, dtype=jnp.int32) // TILE < length
    live_mask = live_pos[:, None] & live_pos[None, :]
    target = source + ladder
    resid = jnp.where(live_mask, target - denominator * own.astype(jnp.float32), jnp.float32(0.0))
    updated = jnp.where(live_mask, target / denominator, jnp.float32(0.0)).astype(jnp.bfloat16)
    count = (length * TILE).astype(jnp.float32) ** 2
    norm_value = jnp.sqrt(jnp.sum(resid * resid) / count + 1e-06)
    return (updated, norm_value)

def reference(lam, drive, order, dom_tiles, dom_len, factors, e_occ, e_virt):
    pair_count = order.shape[0]
    dom_width = DOM_T * TILE
    occ_index = jnp.broadcast_to(jnp.arange(pair_count, dtype=jnp.int32)[:, None], order.shape)
    inverse = jnp.argsort(order, axis=1).astype(jnp.int32)
    partner_slot = inverse[order, occ_index].astype(jnp.int32)
    tile_ids = dom_tiles[occ_index, order]
    lengths = dom_len[occ_index, order]
    occ_pair = e_occ[:, None] + e_occ[order]
    tile_of = jnp.arange(dom_width, dtype=jnp.int32) // TILE
    live_pos = tile_of[None, None, :] < lengths[:, :, None]
    current = jnp.where(live_pos[..., :, None] & live_pos[..., None, :], lam, jnp.zeros_like(lam))
    update_fn = partial(pair_update, factors=factors, e_virt=e_virt)
    norm_list = []
    for step in range(ITERS):
        partner = current[order, partner_slot]
        summed = (current.astype(jnp.float32) + jnp.swapaxes(partner, 2, 3).astype(jnp.float32)).astype(jnp.bfloat16)
        updated, norms = lax.map(update_fn, (flatten_pairs(summed), flatten_pairs(current), flatten_pairs(drive), flatten_pairs(tile_ids), flatten_pairs(lengths), flatten_pairs(occ_pair)))
        current = updated.reshape(lam.shape)
        norm_list.append(norms.reshape(pair_count, pair_count))
    return (current, jnp.stack(norm_list))
```

```python
import functools

import jax
import jax.numpy as jnp
from jax import lax
from jax.experimental import pallas as pl
from jax.experimental.pallas import tpu as pltpu
from jax.sharding import PartitionSpec as P

F32, BF16, I32 = jnp.float32, jnp.bfloat16, jnp.int32
MESH = pl.DeviceIdType.MESH
NZ, NV, NO, T = 8, 32, 16, 128


def host_of(z, c, d, cj, ty):
    if d == 0:
        diag = c == cj
        g = jnp.where(diag, 1, 0)
        t = jnp.where(diag, c, ty)
        return z, 2 * g + t, jnp.where(diag, ty, c)
    if d < 4:
        zh = lax.rem(z + (d >= 2), NZ) if d >= 2 else z
        return zh, 2 * (2 + 4 * (d - 1) + 2 * c + cj) + ty, 0
    if d > 4:
        e = NZ - d
        zh = lax.rem(z + d + (e >= 2), NZ)
        return zh, 2 * (2 + 4 * (e - 1) + 2 * cj + c) + ty, 1
    low = z < 4
    c_low, c_high = jnp.where(low, c, cj), jnp.where(low, cj, c)
    zh = lax.rem(lax.rem(z, 4) + 2 + 4 * c_low, NZ)
    return zh, 2 * (14 + c_high) + ty, jnp.where(low, 0, 1)


def pair_of(zh, v):
    g, t = lax.div(v, 2), lax.rem(v, 2)
    b = jnp.maximum(g - 2, 0)
    d = lax.div(b, 4) + 1
    z_mid = lax.rem(zh + NZ - jnp.where(d >= 2, 1, 0), NZ)
    i_mid = 2 * z_mid + lax.rem(lax.div(b, 2), 2)
    j_mid = 2 * lax.rem(z_mid + d, NZ) + lax.rem(b, 2)
    zl = lax.rem(zh + 6, NZ)
    z_far = lax.rem(zl, 4)
    i_far = 2 * z_far + lax.div(zl, 4)
    j_far = 2 * (z_far + 4) + (g - 14)
    i = jnp.where(g == 0, 2 * zh, jnp.where(g == 1, 2 * zh + t, jnp.where(g >= 14, i_far, i_mid)))
    j = jnp.where(g == 0, 2 * zh + 1, jnp.where(g == 1, 2 * zh + t, jnp.where(g >= 14, j_far, j_mid)))
    return i, j


def kernel(
    lam, drive, order, tiles, lens, factors, e_occ, e_virt,
    out, norms,
    send, recv, buf1, sel, buf2, ev_own, evb, tab_own, tab, tab_s, cur, drv, e_row, e_col, nacc, osend, orecv,
    s_amp, r_amp, s_fac, r_fac, s_ev, r_ev, s_tab, r_tab, s_sel, r_sel, s_out, r_out, l_sem,
):
    p, v = lax.axis_index("pair"), lax.axis_index("virt")
    z, c = lax.div(p, 2), lax.rem(p, 2)
    k_own = lax.div(v, 16)
    host = c == 1
    my_i, my_j = pair_of(z, v)
    my_t = lax.rem(v, 2)
    diag = lax.div(v, 2) == 1

    def remote(src, dst, ss, rs, pp, vv):
        return pltpu.make_async_remote_copy(
            src_ref=src, dst_ref=dst, send_sem=ss, recv_sem=rs,
            device_id={"pair": pp, "virt": vv}, device_id_type=MESH,
        )

    barrier = pltpu.get_barrier_semaphore()

    def greet(pp, vv):
        pl.semaphore_signal(barrier, inc=1, device_id={"pair": pp, "virt": vv}, device_id_type=MESH)

    targets = []
    for d in range(NZ):
        for cj in range(2):
            for h in range(2):
                zh, vh, side = host_of(z, c, d, cj, lax.rem(k_own + h, 2))
                own = jnp.logical_and(host, vh == v) if d < 2 else None
                targets.append((d, cj, h, 2 * zh + 1, vh, side, own))

    def away(own, act):
        if own is None:
            act()
        else:
            pl.when(jnp.logical_not(own))(act)

    @pl.when(host)
    def _():
        @pl.loop(1, NV)
        def _(d):
            greet(p, lax.rem(v + d, NV))

        @pl.loop(1, NO)
        def _(d):
            greet(lax.rem(p + d, NO), v)

        for s in range(2):
            row = my_i if s == 0 else jnp.where(diag, my_i, my_j)

            @pl.loop(0, NV)
            def _(w):
                self_home = jnp.logical_and(row == p, w == v)

                @pl.when(jnp.logical_not(self_home))
                def _():
                    greet(row, w)

    to_self = jnp.int32(0)
    for d, cj, h, pp, vv, side, own in targets:
        away(own, functools.partial(greet, pp, vv))
        if own is not None:
            to_self += own.astype(I32)

    def find(s, found):
        o = order[0, s]
        return tuple(
            jnp.where(o == 2 * lax.rem(z + n // 2, NZ) + n % 2, s, f) for n, f in enumerate(found)
        )

    slots = lax.fori_loop(0, NO, find, (jnp.int32(0),) * NO)
    for n in range(NO):
        own_lam = lam[0, slots[n]].astype(F32)
        own_drive = drive[0, slots[n]]
        for h in range(2):
            cols = slice(h * T, (h + 1) * T)
            send[n, h] = jnp.concatenate([own_lam[:, cols], own_drive[:, cols]], axis=0).astype(BF16)
    lane = lax.broadcasted_iota(I32, (1, T), 1)
    row_table = jnp.zeros((1, T), I32)
    for j in range(NO):
        for k in range(2):
            row_table = jnp.where(lane == 2 * j + k, tiles[0, j, k], row_table)
        row_table = jnp.where(lane == 32 + j, lens[0, j], row_table)
    tab_own[...] = row_table
    ev_own[...] = e_virt[...].astype(F32)

    pl.semaphore_wait(barrier, jnp.where(host, NV + 7 + NV - 1 + 2 * NV, NV + 8) - 2 * to_self)

    q_own, r_own = lax.div(z, 2), lax.rem(z, 2)

    def slice_copy(vv):
        return remote(
            factors.at[0, q_own, pl.ds(pl.multiple_of(64 * r_own, 64), 64)], buf1.at[v], s_fac, r_fac, p, vv
        )

    def ev_copy(vv):
        return remote(ev_own, evb.at[v], s_ev, r_ev, p, vv)

    def tab_copy(dz):
        return remote(tab_own, tab.at[p], s_tab, r_tab, 2 * lax.rem(z + dz, NZ) + 1, v)

    @pl.when(host)
    def _():
        @pl.loop(1, NV)
        def _(d):
            slice_copy(lax.rem(v + d, NV)).start()

        pltpu.make_async_copy(
            factors.at[0, q_own, pl.ds(pl.multiple_of(64 * r_own, 64), 64)], buf1.at[v], r_fac
        ).start()

        @pl.loop(1, NV)
        def _(d):
            ev_copy(lax.rem(v + d, NV)).start()

        pltpu.make_async_copy(ev_own, evb.at[v], r_ev).start()
        pltpu.make_async_copy(tab_own, tab.at[p], r_tab).start()

    @pl.when(jnp.logical_not(host))
    def _():
        tab_copy(0).start()

    for dz in range(1, NZ):
        tab_copy(dz).start()

    def amp_copy(n, h, side, pp, vv):
        return remote(send.at[n, h], recv.at[side, v], s_amp, r_amp, pp, vv)

    for d, cj, h, pp, vv, side, own in targets:
        n = 2 * d + cj
        away(own, lambda: amp_copy(n, h, side, pp, vv).start())
        if own is not None:
            @pl.when(own)
            def _():
                pltpu.make_async_copy(send.at[n, h], recv.at[side, v], r_amp).start()

    @pl.when(host)
    def _():
        pltpu.make_async_copy(tab, tab, r_tab).wait()
        to_smem = pltpu.make_async_copy(tab, tab_s, l_sem)
        to_smem.start()
        to_smem.wait()
        pltpu.make_async_copy(buf1, buf1, r_fac).wait()
        for dz in range(1, NZ):
            zd = lax.rem(z + dz, NZ)
            i, j = pair_of(zd, v)
            for k in range(2):
                sel[dz, k] = buf1[tab_s[i, 0, 2 * j + k]]
            remote(sel.at[dz], buf2.at[:, z], s_sel, r_sel, 2 * zd + 1, v).start()
        own_tiles = [tab_s[my_i, 0, 2 * my_j + k] for k in range(2)]
        for k in range(2):
            sel[0, k] = buf1[own_tiles[k]]
        pltpu.make_async_copy(sel.at[0], buf2.at[:, z], r_sel).start()
        length = tab_s[my_i, 0, 32 + my_j]
        occ = e_occ[my_i] + e_occ[my_j]
        pltpu.make_async_copy(evb, evb, r_ev).wait()
        for k in range(2):
            energy = evb[own_tiles[k]]
            e_row[k] = energy
            e_col[k] = jnp.transpose(jnp.broadcast_to(energy, (T, T)))
        pltpu.make_async_copy(recv, recv, r_amp).wait()
        for s in range(2):
            pieces = recv[s].astype(F32).reshape(NV, 2, 8, T)
            cur[s] = pieces[:, 0].reshape(2, T, T)
            drv[s] = pieces[:, 1].reshape(2, T, T)
        for s in range(2):
            for k in range(2):
                crossed = jnp.where(diag, s, my_t) == 1
                l = jnp.where(crossed, 1 - k, k)
                live = jnp.logical_and(k < length, l < length)
                cur[s, k] = jnp.where(live, cur[s, k], 0.0)

        pltpu.make_async_copy(buf2, buf2, r_sel).wait()

        def block_step(it, ps, pk, qs, qk, l, partner_counts):
            mine, theirs = cur[ps, pk], cur[qs, qk]
            summed = (mine + jnp.transpose(theirs)).astype(BF16)
            right = buf2[l].reshape(4 * T, T)
            left = buf2[pk].reshape(4 * T, T)
            half = lax.dot_general(
                summed, right, (((1,), (1,)), ((), ())), preferred_element_type=F32
            ).astype(BF16)
            ladder = jnp.zeros((T, T), F32)
            for q in range(4):
                ladder += jnp.dot(
                    left[q * T : (q + 1) * T], half[:, q * T : (q + 1) * T], preferred_element_type=F32
                )
            ladder = ladder.astype(BF16).astype(F32)
            live = jnp.logical_and(pk < length, l < length)

            def update(side, block, ladder, den, old):
                target = drv[side, block] + ladder
                resid = jnp.where(live, target - den * old, 0.0)
                new = jnp.where(live, target / den, 0.0).astype(BF16).astype(F32)
                cur[side, block] = new
                return jnp.sum(resid * resid, keepdims=True)

            first = update(ps, pk, ladder, e_col[pk] + e_row[l] - occ, mine)
            second = update(qs, qk, jnp.transpose(ladder), e_col[l] + e_row[pk] - occ, theirs)
            return first, jnp.where(partner_counts, second, 0.0)

        for it in range(2):
            totals = [jnp.zeros((1, 1), F32), jnp.zeros((1, 1), F32)]
            for k in range(2):
                l = jnp.where(jnp.logical_or(diag, my_t == 0), k, 1 - k)
                qs = jnp.where(diag, 0, 1)
                first, second = block_step(it, 0, k, qs, l, l, jnp.logical_not(diag))
                totals = [totals[0] + first, totals[1] + second]
            for s in range(2):
                nacc[it, s] = jnp.broadcast_to(totals[s], (1, T))

            @pl.when(diag)
            def _():
                first, second = block_step(it, 1, 0, 1, 1, 1, True)
                nacc[it, 1] = jnp.broadcast_to(first + second, (1, T))

        sub = lax.broadcasted_iota(I32, (8, T), 0)
        for s in range(2):
            extra = jnp.zeros((8, T), F32)
            for it in range(2):
                total = jnp.broadcast_to(nacc[it, s], (8, T))
                high = total.astype(BF16).astype(F32)
                extra = jnp.where(sub == 2 * it, high, jnp.where(sub == 2 * it + 1, total - high, extra))
            rows = cur[s].reshape(NV, 8, T)
            message = jnp.concatenate([rows, jnp.broadcast_to(extra[None], (NV, 8, T))], axis=1)
            osend[s] = message.astype(BF16)

        def out_copy(s, w):
            row = my_i if s == 0 else jnp.where(diag, my_i, my_j)
            col = my_j if s == 0 else my_i
            half = lax.rem(lax.div(w, 16) + jnp.where(diag, s, my_t), 2)
            return row, orecv.at[col, half], jnp.logical_and(row == p, w == v)

        for s in range(2):
            @pl.loop(0, NV)
            def _(w):
                row, dst, self_home = out_copy(s, w)

                @pl.when(jnp.logical_not(self_home))
                def _():
                    remote(osend.at[s, w], dst, s_out, r_out, row, w).start()

                @pl.when(self_home)
                def _():
                    pltpu.make_async_copy(osend.at[s, w], dst, r_out).start()

    pltpu.make_async_copy(orecv, orecv, r_out).wait()
    totals = [jnp.zeros((1, T), F32), jnp.zeros((1, T), F32)]
    count = jnp.ones((1, T), F32)
    for s in range(NO):
        j = order[0, s]
        pieces = [orecv[j, h].astype(F32) for h in range(2)]
        out[0, s] = jnp.concatenate([piece[:8] for piece in pieces], axis=1).astype(BF16)
        both = pieces[0][8:] + pieces[1][8:]
        totals = [
            jnp.where(lane == s, both[2 * it : 2 * it + 1] + both[2 * it + 1 : 2 * it + 2], totals[it])
            for it in range(2)
        ]
        size = (lens[0, j] * T).astype(F32)
        count = jnp.where(lane == s, size * size, count)
    for it in range(2):
        norms[it] = jnp.sqrt(totals[it] / count + 1e-6)[:, :NO]

    for d, cj, h, pp, vv, side, own in targets:
        away(own, lambda: amp_copy(2 * d + cj, h, side, pp, vv).wait_send())
    for dz in range(1, NZ):
        tab_copy(dz).wait_send()

    @pl.when(jnp.logical_not(host))
    def _():
        tab_copy(0).wait_send()

    @pl.when(host)
    def _():
        @pl.loop(1, NV)
        def _(d):
            slice_copy(lax.rem(v + d, NV)).wait_send()

        @pl.loop(1, NV)
        def _(d):
            ev_copy(lax.rem(v + d, NV)).wait_send()

        for dz in range(1, NZ):
            remote(sel.at[dz], buf2.at[:, z], s_sel, r_sel, p, v).wait_send()
        for s in range(2):
            @pl.loop(0, NV)
            def _(w):
                row = my_i if s == 0 else jnp.where(diag, my_i, my_j)

                @pl.when(jnp.logical_not(jnp.logical_and(row == p, w == v)))
                def _():
                    remote(osend.at[s, w], osend.at[s, w], s_out, r_out, row, w).wait_send()


def shards(lam, drive, order, dom_tiles, dom_len, factors, e_occ, e_virt):
    vmem, smem = pl.BlockSpec(memory_space=pltpu.VMEM), pl.BlockSpec(memory_space=pltpu.SMEM)
    sem = pltpu.SemaphoreType.DMA
    return pl.pallas_call(
        kernel,
        out_shape=(
            jax.ShapeDtypeStruct((1, NO, 8, 2 * T), BF16),
            jax.ShapeDtypeStruct((2, 1, NO), F32),
        ),
        in_specs=[vmem, vmem, smem, smem, smem, pl.BlockSpec(memory_space=pl.ANY), smem, vmem],
        out_specs=(vmem, vmem),
        scratch_shapes=[
            pltpu.VMEM((NO, 2, 16, T), BF16),
            pltpu.VMEM((2, NV, 16, T), BF16),
            pltpu.VMEM((NV, 64, T), BF16),
            pltpu.VMEM((NZ, 2, 64, T), BF16),
            pltpu.VMEM((2, NZ, 64, T), BF16),
            pltpu.VMEM((1, T), F32),
            pltpu.VMEM((NV, 1, T), F32),
            pltpu.VMEM((1, T), I32),
            pltpu.VMEM((NO, 1, T), I32),
            pltpu.SMEM((NO, 1, T), I32),
            pltpu.VMEM((2, 2, T, T), F32),
            pltpu.VMEM((2, 2, T, T), F32),
            pltpu.VMEM((2, 1, T), F32),
            pltpu.VMEM((2, T, T), F32),
            pltpu.VMEM((2, 2, 1, T), F32),
            pltpu.VMEM((2, NV, 16, T), BF16),
            pltpu.VMEM((NO, 2, 16, T), BF16),
        ]
        + [sem] * 13,
        compiler_params=pltpu.CompilerParams(
            collective_id=0, has_side_effects=True, vmem_limit_bytes=24 << 20
        ),
    )(lam, drive, order, dom_tiles, dom_len, factors, e_occ, e_virt)


def solution(mesh):
    return jax.shard_map(
        shards,
        mesh=mesh,
        in_specs=(
            P("pair", None, "virt", None),
            P("pair", None, "virt", None),
            P("pair", None),
            P("pair", None, None),
            P("pair", None),
            P("virt", None, None, None),
            P(),
            P("virt", None),
        ),
        out_specs=(P("pair", None, "virt", None), P(None, "pair", None)),
        check_vma=False,
    )
```

```python
import functools

import jax
import jax.numpy as jnp
from jax import lax
from jax.experimental import pallas as pl
from jax.experimental.pallas import tpu as pltpu
from jax.sharding import PartitionSpec as P

F32, BF16, I32 = jnp.float32, jnp.bfloat16, jnp.int32
MESH = pl.DeviceIdType.MESH
NZ, NV, NO, T = 8, 32, 16, 128
Y_ORDER = (4, 3, 5, 2, 6, 1, 7)
Y_NEAR = (1, 7, 2, 6, 3, 5, 4)


def host_of(z, c, d, cj, ty):
    if d == 0:
        diag = c == cj
        g = jnp.where(diag, 1, 0)
        t = jnp.where(diag, c, ty)
        return z, 2 * g + t, jnp.where(diag, ty, c)
    if d < 4:
        zh = lax.rem(z + (d >= 2), NZ) if d >= 2 else z
        return zh, 2 * (2 + 4 * (d - 1) + 2 * c + cj) + ty, 0
    if d > 4:
        e = NZ - d
        zh = lax.rem(z + d + (e >= 2), NZ)
        return zh, 2 * (2 + 4 * (e - 1) + 2 * cj + c) + ty, 1
    low = z < 4
    c_low, c_high = jnp.where(low, c, cj), jnp.where(low, cj, c)
    zh = lax.rem(lax.rem(z, 4) + 2 + 4 * c_low, NZ)
    return zh, 2 * (14 + c_high) + ty, jnp.where(low, 0, 1)


def pair_of(zh, v):
    g, t = lax.div(v, 2), lax.rem(v, 2)
    b = jnp.maximum(g - 2, 0)
    d = lax.div(b, 4) + 1
    z_mid = lax.rem(zh + NZ - jnp.where(d >= 2, 1, 0), NZ)
    i_mid = 2 * z_mid + lax.rem(lax.div(b, 2), 2)
    j_mid = 2 * lax.rem(z_mid + d, NZ) + lax.rem(b, 2)
    zl = lax.rem(zh + 6, NZ)
    z_far = lax.rem(zl, 4)
    i_far = 2 * z_far + lax.div(zl, 4)
    j_far = 2 * (z_far + 4) + (g - 14)
    i = jnp.where(g == 0, 2 * zh, jnp.where(g == 1, 2 * zh + t, jnp.where(g >= 14, i_far, i_mid)))
    j = jnp.where(g == 0, 2 * zh + 1, jnp.where(g == 1, 2 * zh + t, jnp.where(g >= 14, j_far, j_mid)))
    return i, j


def kernel(
    lam_in, drive_in, order_in, tiles_in, lens_in, factors, e_occ_in, e_virt_in,
    out, norms,
    lam, drive, order, tiles, lens, e_occ, e_virt,
    send, recv, buf1, sel, buf2, ev_own, evb, tab_own, tab, tab_s, cur, drv, den, inv, osend, orecv,
    s_amp, r_amp, s_fac, r_fac, r_line, s_ev, r_ev, s_tab, r_tab, s_sel, r_sel, s_out, r_out, l_sem, in_sems, go,
):
    p, v = lax.axis_index("pair"), lax.axis_index("virt")
    z, c = lax.div(p, 2), lax.rem(p, 2)
    x, y = lax.div(v, 8), lax.rem(v, 8)
    k_own = lax.div(v, 16)
    host = c == 1
    my_i, my_j = pair_of(z, v)
    my_t = lax.rem(v, 2)
    diag = lax.div(v, 2) == 1
    row_1 = jnp.where(diag, my_i, my_j)

    def remote(src, dst, ss, rs, pp, vv):
        return pltpu.make_async_remote_copy(
            src_ref=src, dst_ref=dst, send_sem=ss, recv_sem=rs,
            device_id={"pair": pp, "virt": vv}, device_id_type=MESH,
        )

    def drain(ref, sem):
        pltpu.make_async_copy(ref, ref, sem).wait()

    loads = [
        pltpu.make_async_copy(src, dst, in_sems.at[n])
        for n, (src, dst) in enumerate([
            (tiles_in, tiles), (lens_in, lens), (order_in, order), (lam_in, lam), (drive_in, drive),
            (e_virt_in, e_virt), (e_occ_in, e_occ),
        ])
    ]
    for load in loads:
        load.start()

    barrier = pltpu.get_barrier_semaphore()

    def greet(pp, vv):
        pl.semaphore_signal(barrier, inc=1, device_id={"pair": pp, "virt": vv}, device_id_type=MESH)

    def at_y(dy):
        return 8 * x + lax.rem(y + dy, 8)

    def at_x(dx):
        return 8 * lax.rem(x + dx, 4) + y

    def at_z(dz):
        return 2 * lax.rem(z + dz, NZ) + 1

    @pl.when(host)
    def _():
        for dy in Y_ORDER:
            greet(p, at_y(dy))
        for dx in (2, 1, 3):
            greet(p, at_x(dx))
        for dz in Y_ORDER:
            greet(at_z(dz), v)

        @pl.loop(0, NZ)
        def _(zz):
            greet(2 * zz, v)

        @pl.loop(0, NV)
        def _(w):
            greet(2 * lax.div(my_i, 2), w)
            greet(2 * lax.div(row_1, 2), w)

    targets = []
    for d in range(NZ):
        for cj in range(2):
            for h in range(2):
                zh, vh, side = host_of(z, c, d, cj, lax.rem(k_own + h, 2))
                own = jnp.logical_and(host, vh == v) if d < 2 else None
                targets.append((2 * d + cj, h, 2 * zh + 1, vh, side, own))

    def away(own, act):
        if own is None:
            act()
        else:
            pl.when(jnp.logical_not(own))(act)

    for load in loads[:2]:
        load.wait()
    lane = lax.broadcasted_iota(I32, (1, T), 1)
    row_table = jnp.zeros((1, T), I32)
    for j in range(NO):
        for k in range(2):
            row_table = jnp.where(lane == 2 * j + k, tiles[0, k, j], row_table)
        row_table = jnp.where(lane == 32 + j, lens[0, j], row_table)
    tab_own[...] = row_table

    my_slice = factors.at[0, lax.div(z, 2), pl.ds(pl.multiple_of(64 * lax.rem(z, 2), 64), 64)]

    def tab_copy(dz):
        return remote(tab_own, tab.at[p], s_tab, r_tab, at_z(dz), v)

    @pl.when(host)
    def _():
        pl.semaphore_wait(barrier, 7 + 3 + 7)
        for dy in Y_ORDER:
            remote(my_slice, buf1.at[v], s_fac, r_line.at[dy], p, at_y(dy)).start()
        for dx in (2, 1, 3):
            remote(my_slice, buf1.at[v], s_fac, r_fac, p, at_x(dx)).start()
        pltpu.make_async_copy(my_slice, buf1.at[v], r_fac).start()
        pltpu.make_async_copy(tab_own, tab.at[p], r_tab).start()
        for dz in Y_ORDER:
            tab_copy(dz).start()

    for load in loads[2:]:
        load.wait()
    ev_own[...] = e_virt[...].astype(F32)

    def find(s, found):
        o = order[0, s]
        return tuple(
            jnp.where(o == 2 * lax.rem(z + n // 2, NZ) + n % 2, s, f) for n, f in enumerate(found)
        )

    slots = lax.fori_loop(0, NO, find, (jnp.int32(0),) * NO)
    for n in range(NO):
        own_lam = lam[0, slots[n]].astype(F32)
        own_drive = drive[0, slots[n]]
        for h in range(2):
            cols = slice(h * T, (h + 1) * T)
            send[n, h] = jnp.concatenate([own_lam[:, cols], own_drive[:, cols]], axis=0).astype(BF16)

    @pl.when(host)
    def _():
        for dy in Y_NEAR:
            source = at_y(8 - dy)
            drain(buf1.at[source], r_line.at[dy])
            for dx in (2, 1, 3):
                remote(buf1.at[source], buf1.at[source], s_fac, r_fac, p, at_x(dx)).start()
        pl.semaphore_wait(go, 1)

    @pl.when(jnp.logical_not(host))
    def _():
        pl.semaphore_wait(barrier, NZ + 2 * NV)
        pl.semaphore_signal(go, inc=1, device_id={"pair": p + 1, "virt": v}, device_id_type=MESH)
        tab_copy(0).start()
        for dz in Y_ORDER:
            tab_copy(dz).start()

    def amp_copy(n, h, side, pp, vv):
        return remote(send.at[n, h], recv.at[side, v], s_amp, r_amp, pp, vv)

    def ev_copy(pp, vv):
        return remote(ev_own, evb.at[v], s_ev, r_ev, pp, vv)

    def when_first(side, act):
        if isinstance(side, int):
            if side == 0:
                act()
        else:
            pl.when(side == 0)(act)

    for n, h, pp, vv, side, own in targets:
        def send_away():
            amp_copy(n, h, side, pp, vv).start()
            when_first(side, lambda: ev_copy(pp, vv).start())

        away(own, send_away)
        if own is not None:
            @pl.when(own)
            def _():
                pltpu.make_async_copy(send.at[n, h], recv.at[side, v], r_amp).start()
                when_first(side, lambda: pltpu.make_async_copy(ev_own, evb.at[v], r_ev).start())

    @pl.when(host)
    def _():
        drain(tab, r_tab)
        to_smem = pltpu.make_async_copy(tab, tab_s, l_sem)
        to_smem.start()
        to_smem.wait()
        drain(buf1.at[0 : 1 + 3 * 8], r_fac)
        for dz in Y_ORDER:
            zd = lax.rem(z + dz, NZ)
            i, j = pair_of(zd, v)
            for k in range(2):
                sel[dz, k] = buf1[tab_s[i, 0, 2 * j + k]]
            remote(sel.at[dz], buf2.at[:, z], s_sel, r_sel, 2 * zd + 1, v).start()
        own_tiles = [tab_s[my_i, 0, 2 * my_j + k] for k in range(2)]
        for k in range(2):
            sel[0, k] = buf1[own_tiles[k]]
        pltpu.make_async_copy(sel.at[0], buf2.at[:, z], r_sel).start()
        length = tab_s[my_i, 0, 32 + my_j]
        occ = e_occ[my_i] + e_occ[my_j]
        drain(evb, r_ev)
        e_row = [evb[tile] for tile in own_tiles]
        e_col = [jnp.transpose(jnp.broadcast_to(e, (T, T))) for e in e_row]
        drain(recv, r_amp)

        crossed = jnp.logical_and(jnp.logical_not(diag), my_t == 1)
        couples = [
            (0, 0, jnp.where(diag, 0, 1), jnp.where(crossed, 1, 0)),
            (0, 1, jnp.where(diag, 0, 1), jnp.where(crossed, 0, 1)),
            (1, 0, 1, 1),
        ]

        def alive(pk, l):
            return jnp.logical_and(pk < length, l < length)

        def prepare(o):
            ps, pk, qs, l = couples[o]
            first = recv[ps, pl.ds(16 * pk, 16)].astype(F32).reshape(16, 2, 8, T)
            second = recv[qs, pl.ds(16 * l, 16)].astype(F32).reshape(16, 2, 8, T)
            live = alive(pk, l)
            cur[o, 0] = jnp.where(live, first[:, 0].reshape(T, T), 0.0)
            cur[o, 1] = jnp.where(live, jnp.transpose(second[:, 0].reshape(T, T)), 0.0)
            drv[o, 0] = first[:, 1].reshape(T, T)
            drv[o, 1] = jnp.transpose(second[:, 1].reshape(T, T))
            e_l = jnp.where(l == 0, e_row[0], e_row[1])
            den[o] = e_col[pk] + e_l - occ
            inv[o] = 1.0 / den[o]

        def iterate(o):
            ps, pk, qs, l = couples[o]
            right = buf2[l].reshape(4 * T, T)
            left = buf2[pk].reshape(4 * T, T)
            live = alive(pk, l)
            now = [cur[o, 0], cur[o, 1]]
            squares = []
            for it in range(2):
                half = lax.dot_general(
                    (now[0] + now[1]).astype(BF16), right, (((1,), (1,)), ((), ())),
                    preferred_element_type=F32,
                ).astype(BF16)
                ladder = jnp.zeros((T, T), F32)
                for q in range(4):
                    rows = slice(q * T, (q + 1) * T)
                    ladder += jnp.dot(left[rows], half[:, rows], preferred_element_type=F32)
                ladder = ladder.astype(BF16).astype(F32)
                for n in range(2):
                    target = drv[o, n] + ladder
                    resid = jnp.where(live, target - den[o] * now[n], 0.0)
                    now[n] = jnp.where(live, target * inv[o], 0.0).astype(BF16).astype(F32)
                    squares.append(jnp.sum(resid * resid, keepdims=True))
            return now[0], jnp.transpose(now[1]), squares

        def norm_rows(first, second):
            rows = jnp.zeros((8, T), F32)
            sub = lax.broadcasted_iota(I32, (8, T), 0)
            for it, total in enumerate((first, second)):
                total = jnp.broadcast_to(total, (8, T))
                high = total.astype(BF16).astype(F32)
                rows = jnp.where(sub == 2 * it, high, jnp.where(sub == 2 * it + 1, total - high, rows))
            return jnp.broadcast_to(rows[None], (16, 8, T))

        def post(side, block, values, rows):
            message = jnp.concatenate([values.reshape(16, 8, T), rows], axis=1)
            osend[side, pl.ds(16 * block, 16)] = message.astype(BF16)

        for o in range(2):
            prepare(o)
        pl.when(diag)(lambda: prepare(2))
        drain(buf2, r_sel)
        done = [iterate(o) for o in range(2)]
        sums = [done[0][2][n] + done[1][2][n] for n in range(4)]
        rows = norm_rows(sums[0], sums[2])
        for o in range(2):
            post(0, o, done[o][0], rows)

        @pl.when(jnp.logical_not(diag))
        def _():
            rows = norm_rows(sums[1], sums[3])
            for o in range(2):
                post(1, couples[o][3], done[o][1], rows)

        @pl.when(diag)
        def _():
            first, second, squares = iterate(2)
            rows = norm_rows(squares[0] + squares[1], squares[2] + squares[3])
            post(1, 0, first, rows)
            post(1, 1, second, rows)

        for s in range(2):
            row, col = (my_i, my_j) if s == 0 else (row_1, my_i)

            @pl.loop(0, NV)
            def _(w):
                half = lax.rem(lax.div(w, 16) + jnp.where(diag, s, my_t), 2)
                dst = orecv.at[col, half]
                self_home = jnp.logical_and(row == p, w == v)

                @pl.when(jnp.logical_not(self_home))
                def _():
                    remote(osend.at[s, w], dst, s_out, r_out, row, w).start()

                @pl.when(self_home)
                def _():
                    pltpu.make_async_copy(osend.at[s, w], dst, r_out).start()

    for n, h, pp, vv, side, own in targets:
        def left():
            amp_copy(n, h, side, pp, vv).wait_send()
            when_first(side, lambda: ev_copy(pp, vv).wait_send())

        away(own, left)
    for dz in range(1, NZ):
        tab_copy(dz).wait_send()

    @pl.when(jnp.logical_not(host))
    def _():
        tab_copy(0).wait_send()

    @pl.when(host)
    def _():
        drain(buf1.at[0 : 7 + 3 * 8], s_fac)
        drain(sel.at[0 : NZ - 1], s_sel)
        for s in range(2):
            row = my_i if s == 0 else row_1

            @pl.loop(0, NV)
            def _(w):
                @pl.when(jnp.logical_not(jnp.logical_and(row == p, w == v)))
                def _():
                    remote(osend.at[s, w], osend.at[s, w], s_out, r_out, row, w).wait_send()

    drain(orecv, r_out)
    totals = [jnp.zeros((1, T), F32), jnp.zeros((1, T), F32)]
    count = jnp.ones((1, T), F32)
    for s in range(NO):
        j = order[0, s]
        pieces = [orecv[j, h].astype(F32) for h in range(2)]
        out[0, s] = jnp.concatenate([piece[:8] for piece in pieces], axis=1).astype(BF16)
        both = pieces[0][8:] + pieces[1][8:]
        totals = [
            jnp.where(lane == s, both[2 * it : 2 * it + 1] + both[2 * it + 1 : 2 * it + 2], totals[it])
            for it in range(2)
        ]
        size = (lens[0, j] * T).astype(F32)
        count = jnp.where(lane == s, size * size, count)
    for it in range(2):
        norms[it] = jnp.sqrt(totals[it] / count + 1e-6)[:, :NO]


def shards(lam, drive, order, dom_tiles, dom_len, factors, e_occ, e_virt):
    vmem = pl.BlockSpec(memory_space=pltpu.VMEM)
    sem = pltpu.SemaphoreType.DMA
    return pl.pallas_call(
        kernel,
        out_shape=(
            jax.ShapeDtypeStruct((1, NO, 8, 2 * T), BF16),
            jax.ShapeDtypeStruct((2, 1, NO), F32),
        ),
        in_specs=[pl.BlockSpec(memory_space=pltpu.HBM)] * 8,
        out_specs=(vmem, vmem),
        scratch_shapes=[
            pltpu.VMEM((1, NO, 8, 2 * T), BF16),
            pltpu.VMEM((1, NO, 8, 2 * T), F32),
            pltpu.SMEM((1, NO), I32),
            pltpu.SMEM((1, 2, NO), I32),
            pltpu.SMEM((1, NO), I32),
            pltpu.SMEM((NO,), F32),
            pltpu.VMEM((1, T), BF16),
            pltpu.VMEM((NO, 2, 16, T), BF16),
            pltpu.VMEM((2, NV, 16, T), BF16),
            pltpu.VMEM((NV, 64, T), BF16),
            pltpu.VMEM((NZ, 2, 64, T), BF16),
            pltpu.VMEM((2, NZ, 64, T), BF16),
            pltpu.VMEM((1, T), F32),
            pltpu.VMEM((NV, 1, T), F32),
            pltpu.VMEM((1, T), I32),
            pltpu.VMEM((NO, 1, T), I32),
            pltpu.SMEM((NO, 1, T), I32),
            pltpu.VMEM((3, 2, T, T), F32),
            pltpu.VMEM((3, 2, T, T), F32),
            pltpu.VMEM((3, T, T), F32),
            pltpu.VMEM((3, T, T), F32),
            pltpu.VMEM((2, NV, 16, T), BF16),
            pltpu.VMEM((NO, 2, 16, T), BF16),
        ]
        + [sem] * 4
        + [sem((8,))]
        + [sem] * 9
        + [sem((7,)), pltpu.SemaphoreType.REGULAR],
        compiler_params=pltpu.CompilerParams(
            collective_id=0, has_side_effects=True, vmem_limit_bytes=64 << 20
        ),
    )(lam, drive, order, jnp.swapaxes(dom_tiles, 1, 2), dom_len, factors, e_occ, e_virt)


def solution(mesh):
    return jax.shard_map(
        shards,
        mesh=mesh,
        in_specs=(
            P("pair", None, "virt", None),
            P("pair", None, "virt", None),
            P("pair", None),
            P("pair", None, None),
            P("pair", None),
            P("virt", None, None, None),
            P(),
            P("virt", None),
        ),
        out_specs=(P("pair", None, "virt", None), P(None, "pair", None)),
        check_vma=False,
    )
```

```python
import functools

import jax
import jax.numpy as jnp
from jax import lax
from jax.experimental import pallas as pl
from jax.experimental.pallas import tpu as pltpu
from jax.sharding import PartitionSpec as P

F32, BF16, I32 = jnp.float32, jnp.bfloat16, jnp.int32
MESH = pl.DeviceIdType.MESH
NZ, NV, NO, T = 8, 32, 16, 128
Y_ORDER = (4, 3, 5, 2, 6, 1, 7)
X_ORDER = (2, 1, 3)


def host_of(z, c, d, cj, ty):
    if d == 0:
        diag = c == cj
        g = jnp.where(diag, 1, 0)
        t = jnp.where(diag, c, ty)
        return z, 2 * g + t, jnp.where(diag, ty, c)
    if d < 4:
        zh = lax.rem(z + (d >= 2), NZ) if d >= 2 else z
        return zh, 2 * (2 + 4 * (d - 1) + 2 * c + cj) + ty, 0
    if d > 4:
        e = NZ - d
        zh = lax.rem(z + d + (e >= 2), NZ)
        return zh, 2 * (2 + 4 * (e - 1) + 2 * cj + c) + ty, 1
    low = z < 4
    c_low, c_high = jnp.where(low, c, cj), jnp.where(low, cj, c)
    zh = lax.rem(lax.rem(z, 4) + 2 + 4 * c_low, NZ)
    return zh, 2 * (14 + c_high) + ty, jnp.where(low, 0, 1)


def pair_of(zh, v):
    g, t = lax.div(v, 2), lax.rem(v, 2)
    b = jnp.maximum(g - 2, 0)
    d = lax.div(b, 4) + 1
    z_mid = lax.rem(zh + NZ - jnp.where(d >= 2, 1, 0), NZ)
    i_mid = 2 * z_mid + lax.rem(lax.div(b, 2), 2)
    j_mid = 2 * lax.rem(z_mid + d, NZ) + lax.rem(b, 2)
    zl = lax.rem(zh + 6, NZ)
    z_far = lax.rem(zl, 4)
    i_far = 2 * z_far + lax.div(zl, 4)
    j_far = 2 * (z_far + 4) + (g - 14)
    i = jnp.where(g == 0, 2 * zh, jnp.where(g == 1, 2 * zh + t, jnp.where(g >= 14, i_far, i_mid)))
    j = jnp.where(g == 0, 2 * zh + 1, jnp.where(g == 1, 2 * zh + t, jnp.where(g >= 14, j_far, j_mid)))
    return i, j


def kernel(
    lam_in, drive_in, order_in, tiles_in, lens_in, factors, e_occ_in, e_virt_in,
    out, norms,
    lam, drive, order, tiles, lens, e_occ, e_virt,
    send, recv, buf1, sel, buf2, ev_own, evb, tab_own, tab, tab_s, ids, cur, drv, den, inv, osend, orecv,
    s_amp, r_amp, s_fac, r_fac, s_ev, r_ev, s_tab, r_tab, s_sel, r_sel, s_out, r_out, l_sem, in_sems, go,
):
    p, v = lax.axis_index("pair"), lax.axis_index("virt")
    z, c = lax.div(p, 2), lax.rem(p, 2)
    x, y = lax.div(v, 8), lax.rem(v, 8)
    k_own = lax.div(v, 16)
    host = c == 1
    my_i, my_j = pair_of(z, v)
    my_t = lax.rem(v, 2)
    diag = lax.div(v, 2) == 1
    row_1 = jnp.where(diag, my_i, my_j)

    def remote(src, dst, ss, rs, pp, vv):
        return pltpu.make_async_remote_copy(
            src_ref=src, dst_ref=dst, send_sem=ss, recv_sem=rs,
            device_id={"pair": pp, "virt": vv}, device_id_type=MESH,
        )

    def drain(ref, sem):
        pltpu.make_async_copy(ref, ref, sem).wait()

    loads = [
        pltpu.make_async_copy(src, dst, in_sems.at[n])
        for n, (src, dst) in enumerate([
            (tiles_in, tiles), (lens_in, lens), (order_in, order), (lam_in, lam), (drive_in, drive),
            (e_virt_in, e_virt), (e_occ_in, e_occ),
        ])
    ]
    for load in loads:
        load.start()

    barrier = pltpu.get_barrier_semaphore()

    def greet(pp, vv):
        pl.semaphore_signal(barrier, inc=1, device_id={"pair": pp, "virt": vv}, device_id_type=MESH)

    def at_z(dz):
        return 2 * lax.rem(z + dz, NZ) + 1

    def far_first(step):
        a, b = lax.div(step, 4), lax.rem(step, 4)
        dy = jnp.where(lax.rem(a, 2) == 1, 4 - lax.div(a + 1, 2), 4 + lax.div(a, 2))
        dx = jnp.where(lax.rem(b, 2) == 1, 2 - lax.div(b + 1, 2), 2 + lax.div(b, 2))
        return 8 * lax.rem(x + dx, 4) + lax.rem(y + dy, 8)

    @pl.when(host)
    def _():
        @pl.loop(0, NV - 1)
        def _(step):
            greet(p, far_first(step))

        for dz in Y_ORDER:
            greet(at_z(dz), v)
            greet(at_z(dz) - 1, v)
        greet(p - 1, v)

    targets = []
    for d in range(NZ):
        for cj in range(2):
            for h in range(2):
                zh, vh, side = host_of(z, c, d, cj, lax.rem(k_own + h, 2))
                own = jnp.logical_and(host, vh == v) if d < 2 else None
                targets.append((2 * d + cj, h, 2 * zh + 1, vh, side, own))

    def away(own, act):
        if own is None:
            act()
        else:
            pl.when(jnp.logical_not(own))(act)

    for load in loads[:2]:
        load.wait()
    lane = lax.broadcasted_iota(I32, (1, T), 1)
    row_table = jnp.zeros((1, T), I32)
    for j in range(NO):
        for k in range(2):
            row_table = jnp.where(lane == 2 * j + k, tiles[0, k, j], row_table)
        row_table = jnp.where(lane == 32 + j, lens[0, j], row_table)
    tab_own[...] = row_table

    my_rows = 4 * z + x

    def slice_at(place):
        rows = 4 * z + lax.div(place, 8)
        return factors.at[0, pl.ds(pl.multiple_of(16 * rows, 16), 16)]

    def slice_copy(place):
        return remote(slice_at(place), buf1.at[v], s_fac, r_fac, p, place)

    def tab_copy(dz):
        return remote(tab_own, tab.at[p], s_tab, r_tab, at_z(dz), v)

    @pl.when(host)
    def _():
        pl.semaphore_wait(barrier, NV - 1 + NZ - 1)
        for dz in Y_ORDER:
            tab_copy(dz).start()

        @pl.loop(0, NV - 1)
        def _(step):
            slice_copy(far_first(step)).start()

        pltpu.make_async_copy(slice_at(v), buf1.at[v], r_fac).start()
        pltpu.make_async_copy(tab_own, tab.at[p], r_tab).start()

    @pl.when(jnp.logical_not(host))
    def _():
        pl.semaphore_wait(barrier, NZ)
        for dz in Y_ORDER:
            tab_copy(dz).start()
        tab_copy(0).start()

    for load in loads[2:]:
        load.wait()
    ev_own[...] = e_virt[...].astype(F32)

    def find(s, found):
        o = order[0, s]
        return tuple(
            jnp.where(o == 2 * lax.rem(z + n // 2, NZ) + n % 2, s, f) for n, f in enumerate(found)
        )

    slots = lax.fori_loop(0, NO, find, (jnp.int32(0),) * NO)
    for n in range(NO):
        own_lam = lam[0, slots[n]].astype(F32)
        own_drive = drive[0, slots[n]]
        for h in range(2):
            cols = slice(h * T, (h + 1) * T)
            send[n, h] = jnp.concatenate([own_lam[:, cols], own_drive[:, cols]], axis=0).astype(BF16)

    @pl.when(host)
    def _():
        drain(tab, r_tab)
        pl.semaphore_signal(go, inc=1, device_id={"pair": p - 1, "virt": v}, device_id_type=MESH)

    @pl.when(jnp.logical_not(host))
    def _():
        pl.semaphore_wait(go, 1)

    def amp_copy(n, h, side, pp, vv):
        return remote(send.at[n, h], recv.at[side, v], s_amp, r_amp, pp, vv)

    def ev_copy(pp, vv):
        return remote(ev_own, evb.at[v], s_ev, r_ev, pp, vv)

    def when_first(side, act):
        if isinstance(side, int):
            if side == 0:
                act()
        else:
            pl.when(side == 0)(act)

    for n, h, pp, vv, side, own in targets:
        def send_away():
            amp_copy(n, h, side, pp, vv).start()
            when_first(side, lambda: ev_copy(pp, vv).start())

        away(own, send_away)
        if own is not None:
            @pl.when(own)
            def _():
                pltpu.make_async_copy(send.at[n, h], recv.at[side, v], r_amp).start()
                when_first(side, lambda: pltpu.make_async_copy(ev_own, evb.at[v], r_ev).start())

    @pl.when(host)
    def _():
        to_smem = pltpu.make_async_copy(tab, tab_s, l_sem)
        to_smem.start()
        to_smem.wait()
        places = [
            (lax.rem(z + dz, NZ), 8 * lax.rem(x + dx, 4) + y) for dz in Y_ORDER + (0,) for dx in X_ORDER + (0,)
        ]
        for n, (zd, vd) in enumerate(places):
            i, j = pair_of(zd, vd)
            for k in range(2):
                ids[2 * n + k] = tab_s[i, 0, 2 * j + k]
        own_tiles = [ids[62 + k] for k in range(2)]
        drain(buf1, r_fac)
        for n, (zd, vd) in enumerate(places):
            for k in range(2):
                sel[n, k] = buf1[ids[2 * n + k]]
            if n < 31:
                remote(sel.at[n], buf2.at[:, my_rows], s_sel, r_sel, 2 * zd + 1, vd).start()
            else:
                pltpu.make_async_copy(sel.at[n], buf2.at[:, my_rows], r_sel).start()
        length = tab_s[my_i, 0, 32 + my_j]
        occ = e_occ[my_i] + e_occ[my_j]
        drain(evb, r_ev)
        e_row = [evb[tile] for tile in own_tiles]
        e_col = [jnp.transpose(jnp.broadcast_to(e, (T, T))) for e in e_row]
        drain(recv, r_amp)

        crossed = jnp.logical_and(jnp.logical_not(diag), my_t == 1)
        couples = [
            (0, 0, jnp.where(diag, 0, 1), jnp.where(crossed, 1, 0)),
            (0, 1, jnp.where(diag, 0, 1), jnp.where(crossed, 0, 1)),
            (1, 0, 1, 1),
        ]

        def alive(pk, l):
            return jnp.logical_and(pk < length, l < length)

        def prepare(o):
            ps, pk, qs, l = couples[o]
            first = recv[ps, pl.ds(16 * pk, 16)].astype(F32).reshape(16, 2, 8, T)
            second = recv[qs, pl.ds(16 * l, 16)].astype(F32).reshape(16, 2, 8, T)
            live = alive(pk, l)
            cur[o, 0] = jnp.where(live, first[:, 0].reshape(T, T), 0.0)
            cur[o, 1] = jnp.where(live, jnp.transpose(second[:, 0].reshape(T, T)), 0.0)
            drv[o, 0] = first[:, 1].reshape(T, T)
            drv[o, 1] = jnp.transpose(second[:, 1].reshape(T, T))
            e_l = jnp.where(l == 0, e_row[0], e_row[1])
            den[o] = e_col[pk] + e_l - occ
            inv[o] = 1.0 / den[o]

        def iterate(o):
            ps, pk, qs, l = couples[o]
            right = buf2[l].reshape(4 * T, T)
            left = buf2[pk].reshape(4 * T, T)
            live = alive(pk, l)
            now = [cur[o, 0], cur[o, 1]]
            squares = []
            for it in range(2):
                half = lax.dot_general(
                    (now[0] + now[1]).astype(BF16), right, (((1,), (1,)), ((), ())),
                    preferred_element_type=F32,
                ).astype(BF16)
                ladder = jnp.zeros((T, T), F32)
                for q in range(4):
                    rows = slice(q * T, (q + 1) * T)
                    ladder += jnp.dot(left[rows], half[:, rows], preferred_element_type=F32)
                ladder = ladder.astype(BF16).astype(F32)
                for n in range(2):
                    target = drv[o, n] + ladder
                    resid = jnp.where(live, target - den[o] * now[n], 0.0)
                    now[n] = jnp.where(live, target * inv[o], 0.0).astype(BF16).astype(F32)
                    squares.append(jnp.sum(resid * resid, keepdims=True))
            return now[0], jnp.transpose(now[1]), squares

        def norm_rows(first, second):
            rows = jnp.zeros((8, T), F32)
            sub = lax.broadcasted_iota(I32, (8, T), 0)
            for it, total in enumerate((first, second)):
                total = jnp.broadcast_to(total, (8, T))
                high = total.astype(BF16).astype(F32)
                rows = jnp.where(sub == 2 * it, high, jnp.where(sub == 2 * it + 1, total - high, rows))
            return jnp.broadcast_to(rows[None], (16, 8, T))

        def post(side, block, values, rows):
            message = jnp.concatenate([values.reshape(16, 8, T), rows], axis=1)
            osend[side, pl.ds(16 * block, 16)] = message.astype(BF16)

        for o in range(2):
            prepare(o)
        pl.when(diag)(lambda: prepare(2))
        drain(buf2, r_sel)
        done = [iterate(o) for o in range(2)]
        sums = [done[0][2][n] + done[1][2][n] for n in range(4)]
        rows = norm_rows(sums[0], sums[2])
        for o in range(2):
            post(0, o, done[o][0], rows)

        @pl.when(jnp.logical_not(diag))
        def _():
            rows = norm_rows(sums[1], sums[3])
            for o in range(2):
                post(1, couples[o][3], done[o][1], rows)

        @pl.when(diag)
        def _():
            first, second, squares = iterate(2)
            rows = norm_rows(squares[0] + squares[1], squares[2] + squares[3])
            post(1, 0, first, rows)
            post(1, 1, second, rows)

        for s in range(2):
            row, col = (my_i, my_j) if s == 0 else (row_1, my_i)

            @pl.loop(0, NV)
            def _(w):
                half = lax.rem(lax.div(w, 16) + jnp.where(diag, s, my_t), 2)
                dst = orecv.at[col, half]
                self_home = jnp.logical_and(row == p, w == v)

                @pl.when(jnp.logical_not(self_home))
                def _():
                    remote(osend.at[s, w], dst, s_out, r_out, row, w).start()

                @pl.when(self_home)
                def _():
                    pltpu.make_async_copy(osend.at[s, w], dst, r_out).start()

    for n, h, pp, vv, side, own in targets:
        def left():
            amp_copy(n, h, side, pp, vv).wait_send()
            when_first(side, lambda: ev_copy(pp, vv).wait_send())

        away(own, left)
    for dz in range(1, NZ):
        tab_copy(dz).wait_send()

    @pl.when(jnp.logical_not(host))
    def _():
        tab_copy(0).wait_send()

    @pl.when(host)
    def _():
        drain(buf1.at[0 : NV - 1], s_fac)
        drain(sel.at[0 : NV - 1], s_sel)
        for s in range(2):
            row = my_i if s == 0 else row_1

            @pl.loop(0, NV)
            def _(w):
                @pl.when(jnp.logical_not(jnp.logical_and(row == p, w == v)))
                def _():
                    remote(osend.at[s, w], osend.at[s, w], s_out, r_out, row, w).wait_send()

    drain(orecv, r_out)
    totals = [jnp.zeros((1, T), F32), jnp.zeros((1, T), F32)]
    count = jnp.ones((1, T), F32)
    for s in range(NO):
        j = order[0, s]
        pieces = [orecv[j, h].astype(F32) for h in range(2)]
        out[0, s] = jnp.concatenate([piece[:8] for piece in pieces], axis=1).astype(BF16)
        both = pieces[0][8:] + pieces[1][8:]
        totals = [
            jnp.where(lane == s, both[2 * it : 2 * it + 1] + both[2 * it + 1 : 2 * it + 2], totals[it])
            for it in range(2)
        ]
        size = (lens[0, j] * T).astype(F32)
        count = jnp.where(lane == s, size * size, count)
    for it in range(2):
        norms[it] = jnp.sqrt(totals[it] / count + 1e-6)[:, :NO]


def shards(lam, drive, order, dom_tiles, dom_len, factors, e_occ, e_virt):
    vmem = pl.BlockSpec(memory_space=pltpu.VMEM)
    sem = pltpu.SemaphoreType.DMA
    return pl.pallas_call(
        kernel,
        out_shape=(
            jax.ShapeDtypeStruct((1, NO, 8, 2 * T), BF16),
            jax.ShapeDtypeStruct((2, 1, NO), F32),
        ),
        in_specs=[pl.BlockSpec(memory_space=pltpu.HBM)] * 8,
        out_specs=(vmem, vmem),
        scratch_shapes=[
            pltpu.VMEM((1, NO, 8, 2 * T), BF16),
            pltpu.VMEM((1, NO, 8, 2 * T), F32),
            pltpu.SMEM((1, NO), I32),
            pltpu.SMEM((1, 2, NO), I32),
            pltpu.SMEM((1, NO), I32),
            pltpu.SMEM((NO,), F32),
            pltpu.VMEM((1, T), BF16),
            pltpu.VMEM((NO, 2, 16, T), BF16),
            pltpu.VMEM((2, NV, 16, T), BF16),
            pltpu.VMEM((NV, 16, T), BF16),
            pltpu.VMEM((NV, 2, 16, T), BF16),
            pltpu.VMEM((2, NV, 16, T), BF16),
            pltpu.VMEM((1, T), F32),
            pltpu.VMEM((NV, 1, T), F32),
            pltpu.VMEM((1, T), I32),
            pltpu.VMEM((NO, 1, T), I32),
            pltpu.SMEM((NO, 1, T), I32),
            pltpu.SMEM((2 * NV,), I32),
            pltpu.VMEM((3, 2, T, T), F32),
            pltpu.VMEM((3, 2, T, T), F32),
            pltpu.VMEM((3, T, T), F32),
            pltpu.VMEM((3, T, T), F32),
            pltpu.VMEM((2, NV, 16, T), BF16),
            pltpu.VMEM((NO, 2, 16, T), BF16),
        ]
        + [sem] * 13
        + [sem((7,)), pltpu.SemaphoreType.REGULAR],
        compiler_params=pltpu.CompilerParams(
            collective_id=0, has_side_effects=True, vmem_limit_bytes=64 << 20
        ),
    )(lam, drive, order, jnp.swapaxes(dom_tiles, 1, 2), dom_len, factors.reshape(1, 4 * T, T), e_occ, e_virt)


def solution(mesh):
    return jax.shard_map(
        shards,
        mesh=mesh,
        in_specs=(
            P("pair", None, "virt", None),
            P("pair", None, "virt", None),
            P("pair", None),
            P("pair", None, None),
            P("pair", None),
            P("virt", None, None, None),
            P(),
            P("virt", None),
        ),
        out_specs=(P("pair", None, "virt", None), P(None, "pair", None)),
        check_vma=False,
    )
```

```python
import functools

import jax
import jax.numpy as jnp
from jax import lax
from jax.experimental import pallas as pl
from jax.experimental.pallas import tpu as pltpu
from jax.sharding import PartitionSpec as P

F32, BF16, I32 = jnp.float32, jnp.bfloat16, jnp.int32
MESH = pl.DeviceIdType.MESH
NZ, NV, NO, T = 8, 32, 16, 128
Y_ORDER = (4, 3, 5, 2, 6, 1, 7)


def host_of(i, j, ty):
    diag = i == j
    low, high = jnp.minimum(i, j), jnp.maximum(i, j)
    rank = lax.div(low * (31 - low), 2) + high - low - 1
    plane = jnp.where(diag, lax.div(i, 2), lax.div(rank, 15))
    virt = jnp.where(diag, lax.rem(i, 2), 2 + 2 * lax.rem(rank, 15) + ty)
    return plane, virt, jnp.where(diag, ty, (i > j).astype(I32))


def pair_of(plane, v):
    g = lax.div(v, 2)
    rank = 15 * plane + jnp.maximum(g - 1, 0)
    low = sum((rank >= n * (31 - n) // 2).astype(I32) for n in range(1, 15))
    high = rank - lax.div(low * (31 - low), 2) + low + 1
    own = 2 * plane + lax.rem(v, 2)
    return jnp.where(g == 0, own, low), jnp.where(g == 0, own, high)


def kernel(
    lam_in, drive_in, order_in, tiles_in, lens_in, factors, e_occ_in, e_virt_in,
    out, norms,
    lam, drive, order, tiles, lens, e_occ, e_virt,
    send, recv, buf1, sel, buf2, ev_own, evb, tab_own, tab, tab_s, ids, cur, drv, den, inv, osend, orecv,
    s_amp, r_amp, s_fac, r_fac, s_ev, r_ev, s_tab, r_tab, s_sel, r_sel, s_out, r_out, l_sem, in_sems, column, ready,
):
    p, v = lax.axis_index("pair"), lax.axis_index("virt")
    z, c = lax.div(p, 2), lax.rem(p, 2)
    x, y = lax.div(v, 8), lax.rem(v, 8)
    k_own = lax.div(v, 16)
    host = c == 1
    my_i, my_j = pair_of(z, v)
    my_t = lax.rem(v, 2)
    diag = lax.div(v, 2) == 0
    row_1 = jnp.where(diag, my_i, my_j)

    def remote(src, dst, ss, rs, pp, vv):
        return pltpu.make_async_remote_copy(
            src_ref=src, dst_ref=dst, send_sem=ss, recv_sem=rs,
            device_id={"pair": pp, "virt": vv}, device_id_type=MESH,
        )

    def drain(ref, sem):
        pltpu.make_async_copy(ref, ref, sem).wait()

    loads = [
        pltpu.make_async_copy(src, dst, in_sems.at[n])
        for n, (src, dst) in enumerate([
            (tiles_in, tiles), (lens_in, lens), (order_in, order), (lam_in, lam), (drive_in, drive),
            (e_virt_in, e_virt), (e_occ_in, e_occ),
        ])
    ]
    for load in loads:
        load.start()

    barrier = pltpu.get_barrier_semaphore()

    def greet(pp, vv):
        pl.semaphore_signal(barrier, inc=1, device_id={"pair": pp, "virt": vv}, device_id_type=MESH)

    def at_z(dz):
        return 2 * lax.rem(z + dz, NZ) + 1

    def far_first(step):
        a, b = lax.div(step, 4), lax.rem(step, 4)
        dy = jnp.where(lax.rem(a, 2) == 1, 4 - lax.div(a + 1, 2), 4 + lax.div(a, 2))
        dx = jnp.where(lax.rem(b, 2) == 1, 2 - lax.div(b + 1, 2), 2 + lax.div(b, 2))
        return 8 * lax.rem(x + dx, 4) + lax.rem(y + dy, 8)

    @pl.when(host)
    def _():
        @pl.loop(0, NV - 1)
        def _(step):
            greet(p, far_first(step))

        for dz in Y_ORDER:
            greet(at_z(dz) - 1, v)
        greet(p - 1, v)

    targets = []
    for j in range(NO):
        for h in range(2):
            zh, vh, side = host_of(p, j, lax.rem(k_own + h, 2))
            targets.append((j, h, 2 * zh + 1, vh, side, jnp.logical_and(2 * zh + 1 == p, vh == v)))

    def away(own, act):
        pl.when(jnp.logical_not(own))(act)

    for load in loads[:2]:
        load.wait()
    lane = lax.broadcasted_iota(I32, (1, T), 1)
    row_table = jnp.zeros((1, T), I32)
    for j in range(NO):
        for k in range(2):
            row_table = jnp.where(lane == 2 * j + k, tiles[0, k, j], row_table)
        row_table = jnp.where(lane == 32 + j, lens[0, j], row_table)
    tab_own[...] = row_table

    def slice_at(place):
        return factors.at[0, pl.ds(pl.multiple_of(16 * place, 16), 16)]

    def slice_copy(place):
        return remote(slice_at(place), buf1.at[v], s_fac, r_fac, p, place)

    def tab_copy(dz):
        return remote(tab_own, tab.at[p], s_tab, r_tab, at_z(dz), v)

    def tell(sem, pp):
        pl.semaphore_signal(sem, inc=1, device_id={"pair": pp, "virt": v}, device_id_type=MESH)

    @pl.when(host)
    def _():
        pl.semaphore_wait(barrier, NV - 1)

        @pl.loop(0, NV - 1)
        def _(step):
            slice_copy(far_first(step)).start()

        pltpu.make_async_copy(slice_at(v), buf1.at[v], r_fac).start()
        pltpu.make_async_copy(tab_own, tab.at[p], r_tab).start()

    @pl.when(jnp.logical_not(host))
    def _():
        pl.semaphore_wait(barrier, NZ)
        tell(column, p + 1)
        for dz in Y_ORDER:
            tab_copy(dz).start()
        tab_copy(0).start()

    for load in loads[2:]:
        load.wait()
    ev_own[...] = e_virt[...].astype(F32)

    def find(s, found):
        o = order[0, s]
        return tuple(
            jnp.where(o == n, s, f) for n, f in enumerate(found)
        )

    slots = lax.fori_loop(0, NO, find, (jnp.int32(0),) * NO)
    for n in range(NO):
        own_lam = lam[0, slots[n]].astype(F32)
        own_drive = drive[0, slots[n]]
        for h in range(2):
            cols = slice(h * T, (h + 1) * T)
            send[n, h] = jnp.concatenate([own_lam[:, cols], own_drive[:, cols]], axis=0).astype(BF16)

    @pl.when(host)
    def _():
        pl.semaphore_wait(column, 1)
        for dz in Y_ORDER:
            tell(ready, at_z(dz))
        for dz in Y_ORDER:
            tab_copy(dz).start()
        pl.semaphore_wait(ready, NZ - 1)
        tell(ready, p - 1)

    @pl.when(jnp.logical_not(host))
    def _():
        pl.semaphore_wait(ready, 1)

    def amp_copy(n, h, side, pp, vv):
        return remote(send.at[n, h], recv.at[side, v], s_amp, r_amp, pp, vv)

    def ev_copy(pp, vv):
        return remote(ev_own, evb.at[v], s_ev, r_ev, pp, vv)

    def when_first(side, act):
        pl.when(side == 0)(act)

    for n, h, pp, vv, side, own in targets:
        def send_away():
            amp_copy(n, h, side, pp, vv).start()
            when_first(side, lambda: ev_copy(pp, vv).start())

        away(own, send_away)

        @pl.when(own)
        def _():
            pltpu.make_async_copy(send.at[n, h], recv.at[side, v], r_amp).start()
            when_first(side, lambda: pltpu.make_async_copy(ev_own, evb.at[v], r_ev).start())

    @pl.when(host)
    def _():
        drain(tab, r_tab)
        to_smem = pltpu.make_async_copy(tab, tab_s, l_sem)
        to_smem.start()
        to_smem.wait()

        @pl.loop(0, NV)
        def _(w):
            i, j = pair_of(z, w)
            for k in range(2):
                ids[2 * w + k] = tab_s[i, 0, 2 * j + k]

        own_tiles = [ids[2 * v + k] for k in range(2)]
        drain(buf1, r_fac)

        @pl.loop(0, NV - 1)
        def _(step):
            w = far_first(step)
            for k in range(2):
                sel[w, k] = buf1[ids[2 * w + k]]
            remote(sel.at[w], buf2.at[:, v], s_sel, r_sel, p, w).start()

        for k in range(2):
            sel[v, k] = buf1[own_tiles[k]]
        pltpu.make_async_copy(sel.at[v], buf2.at[:, v], r_sel).start()
        length = tab_s[my_i, 0, 32 + my_j]
        occ = e_occ[my_i] + e_occ[my_j]
        drain(evb, r_ev)
        e_row = [evb[tile] for tile in own_tiles]
        e_col = [jnp.transpose(jnp.broadcast_to(e, (T, T))) for e in e_row]
        drain(recv, r_amp)

        crossed = jnp.logical_and(jnp.logical_not(diag), my_t == 1)
        couples = [
            (0, 0, jnp.where(diag, 0, 1), jnp.where(crossed, 1, 0)),
            (0, 1, jnp.where(diag, 0, 1), jnp.where(crossed, 0, 1)),
            (1, 0, 1, 1),
        ]

        def alive(pk, l):
            return jnp.logical_and(pk < length, l < length)

        def prepare(o):
            ps, pk, qs, l = couples[o]
            first = recv[ps, pl.ds(16 * pk, 16)].astype(F32).reshape(16, 2, 8, T)
            second = recv[qs, pl.ds(16 * l, 16)].astype(F32).reshape(16, 2, 8, T)
            live = alive(pk, l)
            cur[o, 0] = jnp.where(live, first[:, 0].reshape(T, T), 0.0)
            cur[o, 1] = jnp.where(live, jnp.transpose(second[:, 0].reshape(T, T)), 0.0)
            drv[o, 0] = first[:, 1].reshape(T, T)
            drv[o, 1] = jnp.transpose(second[:, 1].reshape(T, T))
            e_l = jnp.where(l == 0, e_row[0], e_row[1])
            den[o] = e_col[pk] + e_l - occ
            inv[o] = 1.0 / den[o]

        def iterate(o):
            ps, pk, qs, l = couples[o]
            right = buf2[l].reshape(4 * T, T)
            left = buf2[pk].reshape(4 * T, T)
            live = alive(pk, l)
            now = [cur[o, 0], cur[o, 1]]
            squares = []
            for it in range(2):
                half = lax.dot_general(
                    (now[0] + now[1]).astype(BF16), right, (((1,), (1,)), ((), ())),
                    preferred_element_type=F32,
                ).astype(BF16)
                ladder = jnp.zeros((T, T), F32)
                for q in range(4):
                    rows = slice(q * T, (q + 1) * T)
                    ladder += jnp.dot(left[rows], half[:, rows], preferred_element_type=F32)
                ladder = ladder.astype(BF16).astype(F32)
                for n in range(2):
                    target = drv[o, n] + ladder
                    resid = jnp.where(live, target - den[o] * now[n], 0.0)
                    now[n] = jnp.where(live, target * inv[o], 0.0).astype(BF16).astype(F32)
                    squares.append(jnp.sum(resid * resid, keepdims=True))
            return now[0], jnp.transpose(now[1]), squares

        def norm_rows(first, second):
            rows = jnp.zeros((8, T), F32)
            sub = lax.broadcasted_iota(I32, (8, T), 0)
            for it, total in enumerate((first, second)):
                total = jnp.broadcast_to(total, (8, T))
                high = total.astype(BF16).astype(F32)
                rows = jnp.where(sub == 2 * it, high, jnp.where(sub == 2 * it + 1, total - high, rows))
            return jnp.broadcast_to(rows[None], (16, 8, T))

        def post(side, block, values, rows):
            message = jnp.concatenate([values.reshape(16, 8, T), rows], axis=1)
            osend[side, pl.ds(16 * block, 16)] = message.astype(BF16)

        for o in range(2):
            prepare(o)
        pl.when(diag)(lambda: prepare(2))
        drain(buf2, r_sel)
        done = [iterate(o) for o in range(2)]
        sums = [done[0][2][n] + done[1][2][n] for n in range(4)]
        rows = norm_rows(sums[0], sums[2])
        for o in range(2):
            post(0, o, done[o][0], rows)

        @pl.when(jnp.logical_not(diag))
        def _():
            rows = norm_rows(sums[1], sums[3])
            for o in range(2):
                post(1, couples[o][3], done[o][1], rows)

        @pl.when(diag)
        def _():
            first, second, squares = iterate(2)
            rows = norm_rows(squares[0] + squares[1], squares[2] + squares[3])
            post(1, 0, first, rows)
            post(1, 1, second, rows)

        for s in range(2):
            row, col = (my_i, my_j) if s == 0 else (row_1, my_i)

            @pl.loop(0, NV)
            def _(w):
                half = lax.rem(lax.div(w, 16) + jnp.where(diag, s, my_t), 2)
                dst = orecv.at[col, half]
                self_home = jnp.logical_and(row == p, w == v)

                @pl.when(jnp.logical_not(self_home))
                def _():
                    remote(osend.at[s, w], dst, s_out, r_out, row, w).start()

                @pl.when(self_home)
                def _():
                    pltpu.make_async_copy(osend.at[s, w], dst, r_out).start()

    for n, h, pp, vv, side, own in targets:
        def left():
            amp_copy(n, h, side, pp, vv).wait_send()
            when_first(side, lambda: ev_copy(pp, vv).wait_send())

        away(own, left)
    for dz in range(1, NZ):
        tab_copy(dz).wait_send()

    @pl.when(jnp.logical_not(host))
    def _():
        tab_copy(0).wait_send()

    @pl.when(host)
    def _():
        drain(buf1.at[0 : NV - 1], s_fac)
        drain(sel.at[0 : NV - 1], s_sel)
        for s in range(2):
            row = my_i if s == 0 else row_1

            @pl.loop(0, NV)
            def _(w):
                @pl.when(jnp.logical_not(jnp.logical_and(row == p, w == v)))
                def _():
                    remote(osend.at[s, w], osend.at[s, w], s_out, r_out, row, w).wait_send()

    drain(orecv, r_out)
    totals = [jnp.zeros((1, T), F32), jnp.zeros((1, T), F32)]
    count = jnp.ones((1, T), F32)
    for s in range(NO):
        j = order[0, s]
        pieces = [orecv[j, h].astype(F32) for h in range(2)]
        out[0, s] = jnp.concatenate([piece[:8] for piece in pieces], axis=1).astype(BF16)
        both = pieces[0][8:] + pieces[1][8:]
        totals = [
            jnp.where(lane == s, both[2 * it : 2 * it + 1] + both[2 * it + 1 : 2 * it + 2], totals[it])
            for it in range(2)
        ]
        size = (lens[0, j] * T).astype(F32)
        count = jnp.where(lane == s, size * size, count)
    for it in range(2):
        norms[it] = jnp.sqrt(totals[it] / count + 1e-6)[:, :NO]


def shards(lam, drive, order, dom_tiles, dom_len, factors, e_occ, e_virt):
    vmem = pl.BlockSpec(memory_space=pltpu.VMEM)
    sem = pltpu.SemaphoreType.DMA
    return pl.pallas_call(
        kernel,
        out_shape=(
            jax.ShapeDtypeStruct((1, NO, 8, 2 * T), BF16),
            jax.ShapeDtypeStruct((2, 1, NO), F32),
        ),
        in_specs=[pl.BlockSpec(memory_space=pltpu.HBM)] * 8,
        out_specs=(vmem, vmem),
        scratch_shapes=[
            pltpu.VMEM((1, NO, 8, 2 * T), BF16),
            pltpu.VMEM((1, NO, 8, 2 * T), F32),
            pltpu.SMEM((1, NO), I32),
            pltpu.SMEM((1, 2, NO), I32),
            pltpu.SMEM((1, NO), I32),
            pltpu.SMEM((NO,), F32),
            pltpu.VMEM((1, T), BF16),
            pltpu.VMEM((NO, 2, 16, T), BF16),
            pltpu.VMEM((2, NV, 16, T), BF16),
            pltpu.VMEM((NV, 16, T), BF16),
            pltpu.VMEM((NV, 2, 16, T), BF16),
            pltpu.VMEM((2, NV, 16, T), BF16),
            pltpu.VMEM((1, T), F32),
            pltpu.VMEM((NV, 1, T), F32),
            pltpu.VMEM((1, T), I32),
            pltpu.VMEM((NO, 1, T), I32),
            pltpu.SMEM((NO, 1, T), I32),
            pltpu.SMEM((2 * NV,), I32),
            pltpu.VMEM((3, 2, T, T), F32),
            pltpu.VMEM((3, 2, T, T), F32),
            pltpu.VMEM((3, T, T), F32),
            pltpu.VMEM((3, T, T), F32),
            pltpu.VMEM((2, NV, 16, T), BF16),
            pltpu.VMEM((NO, 2, 16, T), BF16),
        ]
        + [sem] * 13
        + [sem((7,)), pltpu.SemaphoreType.REGULAR, pltpu.SemaphoreType.REGULAR],
        compiler_params=pltpu.CompilerParams(
            collective_id=0, has_side_effects=True, vmem_limit_bytes=64 << 20
        ),
    )(lam, drive, order, jnp.swapaxes(dom_tiles, 1, 2), dom_len, factors.reshape(1, 4 * T, T), e_occ, e_virt)


def solution(mesh):
    return jax.shard_map(
        shards,
        mesh=mesh,
        in_specs=(
            P("pair", None, "virt", None),
            P("pair", None, "virt", None),
            P("pair", None),
            P("pair", None, None),
            P("pair", None),
            P("virt", None, None, None),
            P(),
            P("virt", None),
        ),
        out_specs=(P("pair", None, "virt", None), P(None, "pair", None)),
        check_vma=False,
    )
```

```python
import functools

import jax
import jax.numpy as jnp
from jax import lax
from jax.experimental import pallas as pl
from jax.experimental.pallas import tpu as pltpu
from jax.sharding import PartitionSpec as P

F32, BF16, I32 = jnp.float32, jnp.bfloat16, jnp.int32
MESH = pl.DeviceIdType.MESH
NZ, NV, NO, T = 8, 32, 16, 128
Y_ORDER = (4, 3, 5, 2, 6, 1, 7)


def host_of(i, j, ty):
    diag = i == j
    low, high = jnp.minimum(i, j), jnp.maximum(i, j)
    rank = lax.div(low * (31 - low), 2) + high - low - 1
    plane = jnp.where(diag, lax.div(i, 2), lax.div(rank, 15))
    virt = jnp.where(diag, lax.rem(i, 2), 2 + 2 * lax.rem(rank, 15) + ty)
    return plane, virt, jnp.where(diag, ty, (i > j).astype(I32))


def pair_of(plane, v):
    g = lax.div(v, 2)
    rank = 15 * plane + jnp.maximum(g - 1, 0)
    low = sum((rank >= n * (31 - n) // 2).astype(I32) for n in range(1, 15))
    high = rank - lax.div(low * (31 - low), 2) + low + 1
    own = 2 * plane + lax.rem(v, 2)
    return jnp.where(g == 0, own, low), jnp.where(g == 0, own, high)


def kernel(
    lam_in, drive_in, order_in, tiles_in, lens_in, factors, e_occ_in, e_virt_in,
    orecv,
    lam, drive, order, tiles, lens, e_occ, e_virt,
    send, recv, buf1, sel, buf2, ev_own, evb, tab_own, tab, tab_s, pairs, cur, drv, den, inv, osend,
    s_amp, r_amp, s_fac, r_fac, s_ev, r_ev, s_tab, r_tab, s_sel, r_sel, s_out, r_out, l_sem, in_sems, column, ready,
):
    p, v = lax.axis_index("pair"), lax.axis_index("virt")
    z, c = lax.div(p, 2), lax.rem(p, 2)
    x, y = lax.div(v, 8), lax.rem(v, 8)
    k_own = lax.div(v, 16)
    host = c == 1
    my_i, my_j = pair_of(z, v)
    my_t = lax.rem(v, 2)
    diag = lax.div(v, 2) == 0
    row_1 = jnp.where(diag, my_i, my_j)

    def remote(src, dst, ss, rs, pp, vv):
        return pltpu.make_async_remote_copy(
            src_ref=src, dst_ref=dst, send_sem=ss, recv_sem=rs,
            device_id={"pair": pp, "virt": vv}, device_id_type=MESH,
        )

    def drain(ref, sem):
        pltpu.make_async_copy(ref, ref, sem).wait()

    loads = [
        pltpu.make_async_copy(src, dst, in_sems.at[n])
        for n, (src, dst) in enumerate([
            (tiles_in, tiles), (lens_in, lens), (order_in, order), (lam_in, lam), (drive_in, drive),
            (e_virt_in, e_virt), (e_occ_in, e_occ),
        ])
    ]
    tab[...] = jnp.zeros_like(tab)

    barrier = pltpu.get_barrier_semaphore()

    def greet(pp, vv):
        pl.semaphore_signal(barrier, inc=1, device_id={"pair": pp, "virt": vv}, device_id_type=MESH)

    def at_z(dz):
        return 2 * lax.rem(z + dz, NZ) + 1

    at_x = [8 * lax.rem(x + dx, 4) for dx in range(4)]
    at_y = [lax.rem(y + dy, 8) for dy in range(8)]
    places = [at_x[dx] + at_y[dy] for dy in Y_ORDER + (0,) for dx in (2, 1, 3, 0)][:-1]

    @pl.when(host)
    def _():
        for place in places:
            greet(p, place)
        for dz in Y_ORDER:
            greet(at_z(dz) - 1, v)
        greet(p - 1, v)

    for load in loads:
        load.start()

    targets = []
    for j in range(NO):
        for h in range(2):
            zh, vh, side = host_of(p, j, lax.rem(k_own + h, 2))
            targets.append((j, h, 2 * zh + 1, vh, side, jnp.logical_and(2 * zh + 1 == p, vh == v)))

    def away(own, act):
        pl.when(jnp.logical_not(own))(act)

    @pl.when(host)
    def _():
        @pl.loop(0, NV)
        def _(w):
            i, j = pair_of(z, w)
            pairs[2 * w] = i
            pairs[2 * w + 1] = 2 * j

    for load in loads[:2]:
        load.wait()
    lane = lax.broadcasted_iota(I32, (1, T), 1)
    row_table = jnp.zeros((1, T), I32)
    for j in range(NO):
        for k in range(2):
            row_table = jnp.where(lane == 2 * j + k, tiles[0, k, j], row_table)
        row_table = jnp.where(lane == 32 + j, lens[0, j], row_table)
    tab_own[...] = row_table

    def slice_at(place):
        return factors.at[0, pl.ds(pl.multiple_of(16 * place, 16), 16)]

    def slice_copy(place):
        return remote(slice_at(place), buf1.at[v], s_fac, r_fac, p, place)

    def ev_copy(place):
        return remote(ev_own, evb.at[v], s_ev, r_ev, p, place)

    def tab_copy(dz):
        return remote(tab_own, tab.at[p], s_tab, r_tab, at_z(dz), v)

    def near_tables(dz, act):
        pl.when(z + dz < NZ)(lambda: act(tab_copy(dz)))

    def send_tables(first):
        for dz in range(first, 4):
            near_tables(dz, lambda copy: copy.start())

    def tell(sem, pp):
        pl.semaphore_signal(sem, inc=1, device_id={"pair": pp, "virt": v}, device_id_type=MESH)

    for load in loads[2:]:
        load.wait()
    ev_own[...] = e_virt[...].astype(F32)

    def find(s, found):
        o = order[0, s]
        return tuple(
            jnp.where(o == n, s, f) for n, f in enumerate(found)
        )

    slots = lax.fori_loop(0, NO, find, (jnp.int32(0),) * NO)
    for n in range(NO):
        own_lam = lam[0, slots[n]].astype(F32)
        own_drive = drive[0, slots[n]]
        for h in range(2):
            cols = slice(h * T, (h + 1) * T)
            send[n, h] = jnp.concatenate([own_lam[:, cols], own_drive[:, cols]], axis=0).astype(BF16)

    @pl.when(host)
    def _():
        pl.semaphore_wait(barrier, NV - 1)

        for place in places:
            slice_copy(place).start()
        for place in places:
            ev_copy(place).start()
        pltpu.make_async_copy(slice_at(v), buf1.at[v], r_fac).start()
        pltpu.make_async_copy(ev_own, evb.at[v], r_ev).start()
        pltpu.make_async_copy(tab_own, tab.at[p], r_tab).start()

    @pl.when(jnp.logical_not(host))
    def _():
        pl.semaphore_wait(barrier, NZ)
        tell(column, p + 1)
        send_tables(0)

    def tile(w, k):
        return tab_s[pairs[2 * w], 0, pairs[2 * w + 1] + k]

    def send_slices():
        drain(buf1, r_fac)
        for w in places:
            for k in range(2):
                sel[w, k] = buf1[tile(w, k)]
            remote(sel.at[w], buf2.at[:, v], s_sel, r_sel, p, w).start()
        for k in range(2):
            sel[v, k] = buf1[tile(v, k)]
        pltpu.make_async_copy(sel.at[v], buf2.at[:, v], r_sel).start()

    early = z < 4

    @pl.when(host)
    def _():
        pl.semaphore_wait(column, 1)
        for dz in Y_ORDER:
            tell(ready, at_z(dz))
        send_tables(1)
        for n in range(1, 5):
            @pl.when(jnp.minimum(z, 3) + 1 == n)
            def _():
                drain(tab.at[0 : 2 * n], r_tab)
        to_smem = pltpu.make_async_copy(tab, tab_s, l_sem)
        to_smem.start()
        to_smem.wait()
        pl.when(early)(send_slices)
        pl.semaphore_wait(ready, NZ - 1)
        tell(ready, p - 1)

    @pl.when(jnp.logical_not(host))
    def _():
        pl.semaphore_wait(ready, 1)

    def amp_copy(n, h, side, pp, vv):
        return remote(send.at[n, h], recv.at[side, v], s_amp, r_amp, pp, vv)

    for n, h, pp, vv, side, own in targets:
        away(own, lambda: amp_copy(n, h, side, pp, vv).start())

        @pl.when(own)
        def _():
            pltpu.make_async_copy(send.at[n, h], recv.at[side, v], r_amp).start()

    @pl.when(host)
    def _():
        pl.when(jnp.logical_not(early))(send_slices)
        own_tiles = [tile(v, k) for k in range(2)]
        length = tab_s[my_i, 0, 32 + my_j]
        occ = e_occ[my_i] + e_occ[my_j]
        drain(evb, r_ev)
        e_row = [evb[tile] for tile in own_tiles]
        e_col = [jnp.transpose(jnp.broadcast_to(e, (T, T))) for e in e_row]
        drain(recv, r_amp)

        crossed = jnp.logical_and(jnp.logical_not(diag), my_t == 1)
        couples = [
            (0, 0, jnp.where(diag, 0, 1), jnp.where(crossed, 1, 0)),
            (0, 1, jnp.where(diag, 0, 1), jnp.where(crossed, 0, 1)),
            (1, 0, 1, 1),
        ]

        def alive(pk, l):
            return jnp.logical_and(pk < length, l < length)

        def prepare(o):
            ps, pk, qs, l = couples[o]
            first = recv[ps, pl.ds(16 * pk, 16)].astype(F32).reshape(16, 2, 8, T)
            second = recv[qs, pl.ds(16 * l, 16)].astype(F32).reshape(16, 2, 8, T)
            live = alive(pk, l)
            cur[o, 0] = jnp.where(live, first[:, 0].reshape(T, T), 0.0)
            cur[o, 1] = jnp.where(live, jnp.transpose(second[:, 0].reshape(T, T)), 0.0)
            drv[o, 0] = first[:, 1].reshape(T, T)
            drv[o, 1] = jnp.transpose(second[:, 1].reshape(T, T))
            e_l = jnp.where(l == 0, e_row[0], e_row[1])
            den[o] = e_col[pk] + e_l - occ
            inv[o] = 1.0 / den[o]

        def iterate(o):
            ps, pk, qs, l = couples[o]
            right = buf2[l].reshape(4 * T, T)
            left = buf2[pk].reshape(4 * T, T)
            live = alive(pk, l)
            now = [cur[o, 0], cur[o, 1]]
            squares = []
            for it in range(2):
                half = lax.dot_general(
                    (now[0] + now[1]).astype(BF16), right, (((1,), (1,)), ((), ())),
                    preferred_element_type=F32,
                ).astype(BF16)
                ladder = jnp.zeros((T, T), F32)
                for q in range(4):
                    rows = slice(q * T, (q + 1) * T)
                    ladder += jnp.dot(left[rows], half[:, rows], preferred_element_type=F32)
                ladder = ladder.astype(BF16).astype(F32)
                for n in range(2):
                    target = drv[o, n] + ladder
                    resid = jnp.where(live, target - den[o] * now[n], 0.0)
                    now[n] = jnp.where(live, target * inv[o], 0.0).astype(BF16).astype(F32)
                    squares.append(jnp.sum(resid * resid, keepdims=True))
            return now[0], jnp.transpose(now[1]), squares

        def norm_rows(first, second):
            rows = jnp.zeros((8, T), F32)
            sub = lax.broadcasted_iota(I32, (8, T), 0)
            for it, total in enumerate((first, second)):
                total = jnp.broadcast_to(total, (8, T))
                high = total.astype(BF16).astype(F32)
                rows = jnp.where(sub == 2 * it, high, jnp.where(sub == 2 * it + 1, total - high, rows))
            return jnp.broadcast_to(rows[None], (16, 8, T))

        def post(side, block, values, rows):
            message = jnp.concatenate([values.reshape(16, 8, T), rows], axis=1)
            osend[side, pl.ds(16 * block, 16)] = message.astype(BF16)

        for o in range(2):
            prepare(o)
        pl.when(diag)(lambda: prepare(2))
        drain(buf2, r_sel)
        done = [iterate(o) for o in range(2)]
        sums = [done[0][2][n] + done[1][2][n] for n in range(4)]
        rows = norm_rows(sums[0], sums[2])
        for o in range(2):
            post(0, o, done[o][0], rows)

        @pl.when(jnp.logical_not(diag))
        def _():
            rows = norm_rows(sums[1], sums[3])
            for o in range(2):
                post(1, couples[o][3], done[o][1], rows)

        @pl.when(diag)
        def _():
            first, second, squares = iterate(2)
            rows = norm_rows(squares[0] + squares[1], squares[2] + squares[3])
            post(1, 0, first, rows)
            post(1, 1, second, rows)

        for s in range(2):
            row, col = (my_i, my_j) if s == 0 else (row_1, my_i)

            @pl.loop(0, NV)
            def _(w):
                half = lax.rem(lax.div(w, 16) + jnp.where(diag, s, my_t), 2)
                dst = orecv.at[col, half]
                self_home = jnp.logical_and(row == p, w == v)

                @pl.when(jnp.logical_not(self_home))
                def _():
                    remote(osend.at[s, w], dst, s_out, r_out, row, w).start()

                @pl.when(self_home)
                def _():
                    pltpu.make_async_copy(osend.at[s, w], dst, r_out).start()

    for n, h, pp, vv, side, own in targets:
        away(own, lambda: amp_copy(n, h, side, pp, vv).wait_send())
    for dz in range(1, 4):
        near_tables(dz, lambda copy: copy.wait_send())

    @pl.when(jnp.logical_not(host))
    def _():
        tab_copy(0).wait_send()

    @pl.when(host)
    def _():
        drain(buf1.at[0 : NV - 1], s_fac)
        drain(evb.at[0 : NV - 1], s_ev)
        drain(sel.at[0 : NV - 1], s_sel)
        for s in range(2):
            row = my_i if s == 0 else row_1

            @pl.loop(0, NV)
            def _(w):
                @pl.when(jnp.logical_not(jnp.logical_and(row == p, w == v)))
                def _():
                    remote(osend.at[s, w], osend.at[s, w], s_out, r_out, row, w).wait_send()

    drain(orecv, r_out)


def unpack(orecv, order, lens, out, norms):
    lane = lax.broadcasted_iota(I32, (1, T), 1)
    totals = [jnp.zeros((1, T), F32), jnp.zeros((1, T), F32)]
    count = jnp.ones((1, T), F32)
    for s in range(NO):
        j = order[0, s]
        pieces = [orecv[j, h].astype(F32) for h in range(2)]
        out[0, s] = jnp.concatenate([piece[:8] for piece in pieces], axis=1).astype(BF16)
        both = pieces[0][8:] + pieces[1][8:]
        totals = [
            jnp.where(lane == s, both[2 * it : 2 * it + 1] + both[2 * it + 1 : 2 * it + 2], totals[it])
            for it in range(2)
        ]
        size = (lens[0, j] * T).astype(F32)
        count = jnp.where(lane == s, size * size, count)
    for it in range(2):
        norms[it] = jnp.sqrt(totals[it] / count + 1e-6)[:, :NO]


def shards(lam, drive, order, dom_tiles, dom_len, factors, e_occ, e_virt):
    vmem, smem = pl.BlockSpec(memory_space=pltpu.VMEM), pl.BlockSpec(memory_space=pltpu.SMEM)
    hbm = pl.BlockSpec(memory_space=pltpu.HBM)
    sem = pltpu.SemaphoreType.DMA
    pieces = pl.pallas_call(
        kernel,
        out_shape=jax.ShapeDtypeStruct((NO, 2, 16, T), BF16),
        in_specs=[hbm] * 8,
        out_specs=hbm,
        scratch_shapes=[
            pltpu.VMEM((1, NO, 8, 2 * T), BF16),
            pltpu.VMEM((1, NO, 8, 2 * T), F32),
            pltpu.SMEM((1, NO), I32),
            pltpu.SMEM((1, 2, NO), I32),
            pltpu.SMEM((1, NO), I32),
            pltpu.SMEM((NO,), F32),
            pltpu.VMEM((1, T), BF16),
            pltpu.VMEM((NO, 2, 16, T), BF16),
            pltpu.VMEM((2, NV, 16, T), BF16),
            pltpu.VMEM((NV, 16, T), BF16),
            pltpu.VMEM((NV, 2, 16, T), BF16),
            pltpu.VMEM((2, NV, 16, T), BF16),
            pltpu.VMEM((1, T), F32),
            pltpu.VMEM((NV, 1, T), F32),
            pltpu.VMEM((1, T), I32),
            pltpu.VMEM((NO, 1, T), I32),
            pltpu.SMEM((NO, 1, T), I32),
            pltpu.SMEM((2 * NV,), I32),
            pltpu.VMEM((3, 2, T, T), F32),
            pltpu.VMEM((3, 2, T, T), F32),
            pltpu.VMEM((3, T, T), F32),
            pltpu.VMEM((3, T, T), F32),
            pltpu.VMEM((2, NV, 16, T), BF16),
        ]
        + [sem] * 13
        + [sem((7,)), pltpu.SemaphoreType.REGULAR, pltpu.SemaphoreType.REGULAR],
        compiler_params=pltpu.CompilerParams(
            collective_id=0, has_side_effects=True, vmem_limit_bytes=64 << 20
        ),
    )(lam, drive, order, jnp.swapaxes(dom_tiles, 1, 2), dom_len, factors.reshape(1, 4 * T, T), e_occ, e_virt)
    return pl.pallas_call(
        unpack,
        out_shape=(
            jax.ShapeDtypeStruct((1, NO, 8, 2 * T), BF16),
            jax.ShapeDtypeStruct((2, 1, NO), F32),
        ),
        in_specs=[vmem, smem, smem],
        out_specs=(vmem, vmem),
        compiler_params=pltpu.CompilerParams(vmem_limit_bytes=64 << 20),
    )(pieces, order, dom_len)


def solution(mesh):
    return jax.shard_map(
        shards,
        mesh=mesh,
        in_specs=(
            P("pair", None, "virt", None),
            P("pair", None, "virt", None),
            P("pair", None),
            P("pair", None, None),
            P("pair", None),
            P("virt", None, None, None),
            P(),
            P("virt", None),
        ),
        out_specs=(P("pair", None, "virt", None), P(None, "pair", None)),
        check_vma=False,
    )
```

```python
import functools

import jax
import jax.numpy as jnp
from jax import lax
from jax.experimental import pallas as pl
from jax.experimental.pallas import tpu as pltpu
from jax.sharding import PartitionSpec as P

F32, BF16, I32 = jnp.float32, jnp.bfloat16, jnp.int32
MESH = pl.DeviceIdType.MESH
NZ, NV, NO, T = 8, 32, 16, 128
EARLY = 4
Y_ORDER = (4, 3, 5, 2, 6, 1, 7)


def host_of(i, j, ty):
    diag = i == j
    low, high = jnp.minimum(i, j), jnp.maximum(i, j)
    rank = lax.div(low * (31 - low), 2) + high - low - 1
    plane = jnp.where(diag, lax.div(i, 2), lax.div(rank, 15))
    virt = jnp.where(diag, lax.rem(i, 2), 2 + 2 * lax.rem(rank, 15) + ty)
    return plane, virt, jnp.where(diag, ty, (i > j).astype(I32))


def pair_of(plane, v):
    g = lax.div(v, 2)
    rank = 15 * plane + jnp.maximum(g - 1, 0)
    low = sum((rank >= n * (31 - n) // 2).astype(I32) for n in range(1, 15))
    high = rank - lax.div(low * (31 - low), 2) + low + 1
    own = 2 * plane + lax.rem(v, 2)
    return jnp.where(g == 0, own, low), jnp.where(g == 0, own, high)


def kernel(
    lam_in, drive_in, order_in, tiles_in, lens_in, factors, e_occ_in, e_virt_in,
    orecv,
    lam, drive, order, tiles, lens, e_occ, e_virt,
    send, recv, buf1, sel, buf2, ev_own, evb, tab_own, tab, tab_s, pairs, cur, drv, den, inv, osend,
    s_amp, r_amp, s_fac, r_fac, s_ev, r_ev, s_tab, r_tab, s_sel, r_sel, s_out, r_out, l_sem, in_sems, column, ready,
):
    p, v = lax.axis_index("pair"), lax.axis_index("virt")
    z, c = lax.div(p, 2), lax.rem(p, 2)
    x, y = lax.div(v, 8), lax.rem(v, 8)
    k_own = lax.div(v, 16)
    host = c == 1
    my_i, my_j = pair_of(z, v)
    my_t = lax.rem(v, 2)
    diag = lax.div(v, 2) == 0
    row_1 = jnp.where(diag, my_i, my_j)
    early = z < EARLY

    def remote(src, dst, ss, rs, pp, vv):
        return pltpu.make_async_remote_copy(
            src_ref=src, dst_ref=dst, send_sem=ss, recv_sem=rs,
            device_id={"pair": pp, "virt": vv}, device_id_type=MESH,
        )

    def drain(ref, sem):
        pltpu.make_async_copy(ref, ref, sem).wait()

    loads = [
        pltpu.make_async_copy(src, dst, in_sems.at[n])
        for n, (src, dst) in enumerate([
            (tiles_in, tiles), (lens_in, lens), (order_in, order), (lam_in, lam), (drive_in, drive),
            (e_virt_in, e_virt), (e_occ_in, e_occ),
        ])
    ]
    tab[...] = jnp.zeros_like(tab)

    barrier = pltpu.get_barrier_semaphore()

    def greet(pp, vv):
        pl.semaphore_signal(barrier, inc=1, device_id={"pair": pp, "virt": vv}, device_id_type=MESH)

    def at_z(dz):
        return 2 * lax.rem(z + dz, NZ) + 1

    at_x = [8 * lax.rem(x + dx, 4) for dx in range(4)]
    at_y = [lax.rem(y + dy, 8) for dy in range(8)]
    places = [at_x[dx] + at_y[dy] for dy in Y_ORDER + (0,) for dx in (2, 1, 3, 0)][:-1]

    @pl.when(host)
    def _():
        for place in places:
            greet(p, place)
        for dz in Y_ORDER:
            greet(at_z(dz) - 1, v)
        greet(p - 1, v)

        @pl.when(early)
        def _():
            @pl.loop(0, NV)
            def _(w):
                for row in (my_i, row_1):
                    greet(2 * lax.div(row, 2), w)

    for load in loads:
        load.start()

    targets = []
    for j in range(NO):
        for h in range(2):
            zh, vh, side = host_of(p, j, lax.rem(k_own + h, 2))
            own = jnp.logical_and(2 * zh + 1 == p, vh == v)
            targets.append((j, h, 2 * zh + 1, vh, side, own, zh < EARLY))
    greetings = NZ
    for j in range(NO):
        for row in range(2):
            greetings += 2 * (host_of(2 * z + row, j, 0)[0] < EARLY).astype(I32)

    def away(own, act):
        pl.when(jnp.logical_not(own))(act)

    @pl.when(host)
    def _():
        @pl.loop(0, NV)
        def _(w):
            i, j = pair_of(z, w)
            pairs[2 * w] = i
            pairs[2 * w + 1] = 2 * j

    for load in loads[:2]:
        load.wait()
    lane = lax.broadcasted_iota(I32, (1, T), 1)
    row_table = jnp.zeros((1, T), I32)
    for j in range(NO):
        for k in range(2):
            row_table = jnp.where(lane == 2 * j + k, tiles[0, k, j], row_table)
        row_table = jnp.where(lane == 32 + j, lens[0, j], row_table)
    tab_own[...] = row_table

    def slice_at(place):
        return factors.at[0, pl.ds(pl.multiple_of(16 * place, 16), 16)]

    def slice_copy(place):
        return remote(slice_at(place), buf1.at[v], s_fac, r_fac, p, place)

    def ev_copy(place):
        return remote(ev_own, evb.at[v], s_ev, r_ev, p, place)

    def tab_copy(dz):
        return remote(tab_own, tab.at[p], s_tab, r_tab, at_z(dz), v)

    def near_tables(dz, act):
        pl.when(z + dz < NZ)(lambda: act(tab_copy(dz)))

    def send_tables(first):
        for dz in range(first, 4):
            near_tables(dz, lambda copy: copy.start())

    def tell(sem, pp):
        pl.semaphore_signal(sem, inc=1, device_id={"pair": pp, "virt": v}, device_id_type=MESH)

    for load in loads[2:]:
        load.wait()
    ev_own[...] = e_virt[...].astype(F32)

    def find(s, found):
        o = order[0, s]
        return tuple(
            jnp.where(o == n, s, f) for n, f in enumerate(found)
        )

    slots = lax.fori_loop(0, NO, find, (jnp.int32(0),) * NO)
    for n in range(NO):
        own_lam = lam[0, slots[n]].astype(F32)
        own_drive = drive[0, slots[n]]
        for h in range(2):
            cols = slice(h * T, (h + 1) * T)
            send[n, h] = jnp.concatenate([own_lam[:, cols], own_drive[:, cols]], axis=0).astype(BF16)

    def amp_copy(n, h, side, pp, vv):
        return remote(send.at[n, h], recv.at[side, v], s_amp, r_amp, pp, vv)

    def send_amplitudes(to_early):
        for n, h, pp, vv, side, own, at_early in targets:
            now = at_early if to_early else jnp.logical_not(at_early)

            @pl.when(jnp.logical_and(now, jnp.logical_not(own)))
            def _():
                amp_copy(n, h, side, pp, vv).start()

            @pl.when(jnp.logical_and(now, own))
            def _():
                pltpu.make_async_copy(send.at[n, h], recv.at[side, v], r_amp).start()

    @pl.when(host)
    def _():
        pl.semaphore_wait(barrier, NV - 1)

        for place in places:
            slice_copy(place).start()
        for place in places:
            ev_copy(place).start()
        pltpu.make_async_copy(slice_at(v), buf1.at[v], r_fac).start()
        pltpu.make_async_copy(ev_own, evb.at[v], r_ev).start()
        pltpu.make_async_copy(tab_own, tab.at[p], r_tab).start()

    @pl.when(jnp.logical_not(host))
    def _():
        pl.semaphore_wait(barrier, greetings)
        tell(column, p + 1)
        send_tables(0)
        send_amplitudes(True)

    def tile(w, k):
        return tab_s[pairs[2 * w], 0, pairs[2 * w + 1] + k]

    def send_slices():
        drain(buf1, r_fac)
        for w in places:
            for k in range(2):
                sel[w, k] = buf1[tile(w, k)]
            remote(sel.at[w], buf2.at[:, v], s_sel, r_sel, p, w).start()
        for k in range(2):
            sel[v, k] = buf1[tile(v, k)]
        pltpu.make_async_copy(sel.at[v], buf2.at[:, v], r_sel).start()

    @pl.when(host)
    def _():
        pl.semaphore_wait(column, 1)
        for dz in Y_ORDER:
            tell(ready, at_z(dz))
        send_tables(1)
        send_amplitudes(True)
        for n in range(1, 5):
            @pl.when(jnp.minimum(z, 3) + 1 == n)
            def _():
                drain(tab.at[0 : 2 * n], r_tab)
        to_smem = pltpu.make_async_copy(tab, tab_s, l_sem)
        to_smem.start()
        to_smem.wait()
        pl.when(early)(send_slices)
        pl.semaphore_wait(ready, NZ - 1)
        tell(ready, p - 1)

    @pl.when(jnp.logical_not(host))
    def _():
        pl.semaphore_wait(ready, 1)

    send_amplitudes(False)

    @pl.when(host)
    def _():
        pl.when(jnp.logical_not(early))(send_slices)
        own_tiles = [tile(v, k) for k in range(2)]
        length = tab_s[my_i, 0, 32 + my_j]
        occ = e_occ[my_i] + e_occ[my_j]
        drain(evb, r_ev)
        e_row = [evb[tile] for tile in own_tiles]
        e_col = [jnp.transpose(jnp.broadcast_to(e, (T, T))) for e in e_row]
        drain(recv, r_amp)

        crossed = jnp.logical_and(jnp.logical_not(diag), my_t == 1)
        couples = [
            (0, 0, jnp.where(diag, 0, 1), jnp.where(crossed, 1, 0)),
            (0, 1, jnp.where(diag, 0, 1), jnp.where(crossed, 0, 1)),
            (1, 0, 1, 1),
        ]

        def alive(pk, l):
            return jnp.logical_and(pk < length, l < length)

        def prepare(o):
            ps, pk, qs, l = couples[o]
            first = recv[ps, pl.ds(16 * pk, 16)].astype(F32).reshape(16, 2, 8, T)
            second = recv[qs, pl.ds(16 * l, 16)].astype(F32).reshape(16, 2, 8, T)
            live = alive(pk, l)
            cur[o, 0] = jnp.where(live, first[:, 0].reshape(T, T), 0.0)
            cur[o, 1] = jnp.where(live, jnp.transpose(second[:, 0].reshape(T, T)), 0.0)
            drv[o, 0] = first[:, 1].reshape(T, T)
            drv[o, 1] = jnp.transpose(second[:, 1].reshape(T, T))
            e_l = jnp.where(l == 0, e_row[0], e_row[1])
            den[o] = e_col[pk] + e_l - occ
            inv[o] = 1.0 / den[o]

        def iterate(o):
            ps, pk, qs, l = couples[o]
            right = buf2[l].reshape(4 * T, T)
            left = buf2[pk].reshape(4 * T, T)
            live = alive(pk, l)
            now = [cur[o, 0], cur[o, 1]]
            squares = []
            for it in range(2):
                half = lax.dot_general(
                    (now[0] + now[1]).astype(BF16), right, (((1,), (1,)), ((), ())),
                    preferred_element_type=F32,
                ).astype(BF16)
                ladder = jnp.zeros((T, T), F32)
                for q in range(4):
                    rows = slice(q * T, (q + 1) * T)
                    ladder += jnp.dot(left[rows], half[:, rows], preferred_element_type=F32)
                ladder = ladder.astype(BF16).astype(F32)
                for n in range(2):
                    target = drv[o, n] + ladder
                    resid = jnp.where(live, target - den[o] * now[n], 0.0)
                    now[n] = jnp.where(live, target * inv[o], 0.0).astype(BF16).astype(F32)
                    squares.append(jnp.sum(resid * resid, keepdims=True))
            return now[0], jnp.transpose(now[1]), squares

        def norm_rows(first, second):
            rows = jnp.zeros((8, T), F32)
            sub = lax.broadcasted_iota(I32, (8, T), 0)
            for it, total in enumerate((first, second)):
                total = jnp.broadcast_to(total, (8, T))
                high = total.astype(BF16).astype(F32)
                rows = jnp.where(sub == 2 * it, high, jnp.where(sub == 2 * it + 1, total - high, rows))
            return jnp.broadcast_to(rows[None], (16, 8, T))

        def post(side, block, values, rows):
            message = jnp.concatenate([values.reshape(16, 8, T), rows], axis=1)
            osend[side, pl.ds(16 * block, 16)] = message.astype(BF16)

        for o in range(2):
            prepare(o)
        pl.when(diag)(lambda: prepare(2))
        drain(buf2, r_sel)
        done = [iterate(o) for o in range(2)]
        sums = [done[0][2][n] + done[1][2][n] for n in range(4)]
        rows = norm_rows(sums[0], sums[2])
        for o in range(2):
            post(0, o, done[o][0], rows)

        @pl.when(jnp.logical_not(diag))
        def _():
            rows = norm_rows(sums[1], sums[3])
            for o in range(2):
                post(1, couples[o][3], done[o][1], rows)

        @pl.when(diag)
        def _():
            first, second, squares = iterate(2)
            rows = norm_rows(squares[0] + squares[1], squares[2] + squares[3])
            post(1, 0, first, rows)
            post(1, 1, second, rows)

        for s in range(2):
            row, col = (my_i, my_j) if s == 0 else (row_1, my_i)

            @pl.loop(0, NV)
            def _(w):
                half = lax.rem(lax.div(w, 16) + jnp.where(diag, s, my_t), 2)
                dst = orecv.at[col, half]
                self_home = jnp.logical_and(row == p, w == v)

                @pl.when(jnp.logical_not(self_home))
                def _():
                    remote(osend.at[s, w], dst, s_out, r_out, row, w).start()

                @pl.when(self_home)
                def _():
                    pltpu.make_async_copy(osend.at[s, w], dst, r_out).start()

    for n, h, pp, vv, side, own, _ in targets:
        away(own, lambda: amp_copy(n, h, side, pp, vv).wait_send())
    for dz in range(1, 4):
        near_tables(dz, lambda copy: copy.wait_send())

    @pl.when(jnp.logical_not(host))
    def _():
        tab_copy(0).wait_send()

    @pl.when(host)
    def _():
        drain(buf1.at[0 : NV - 1], s_fac)
        drain(evb.at[0 : NV - 1], s_ev)
        drain(sel.at[0 : NV - 1], s_sel)
        for s in range(2):
            row = my_i if s == 0 else row_1

            @pl.loop(0, NV)
            def _(w):
                @pl.when(jnp.logical_not(jnp.logical_and(row == p, w == v)))
                def _():
                    remote(osend.at[s, w], osend.at[s, w], s_out, r_out, row, w).wait_send()

    drain(orecv, r_out)


def unpack(orecv, order, lens, out, norms):
    lane = lax.broadcasted_iota(I32, (1, T), 1)
    totals = [jnp.zeros((1, T), F32), jnp.zeros((1, T), F32)]
    count = jnp.ones((1, T), F32)
    for s in range(NO):
        j = order[0, s]
        pieces = [orecv[j, h].astype(F32) for h in range(2)]
        out[0, s] = jnp.concatenate([piece[:8] for piece in pieces], axis=1).astype(BF16)
        both = pieces[0][8:] + pieces[1][8:]
        totals = [
            jnp.where(lane == s, both[2 * it : 2 * it + 1] + both[2 * it + 1 : 2 * it + 2], totals[it])
            for it in range(2)
        ]
        size = (lens[0, j] * T).astype(F32)
        count = jnp.where(lane == s, size * size, count)
    for it in range(2):
        norms[it] = jnp.sqrt(totals[it] / count + 1e-6)[:, :NO]


def shards(lam, drive, order, dom_tiles, dom_len, factors, e_occ, e_virt):
    vmem, smem = pl.BlockSpec(memory_space=pltpu.VMEM), pl.BlockSpec(memory_space=pltpu.SMEM)
    hbm = pl.BlockSpec(memory_space=pltpu.HBM)
    sem = pltpu.SemaphoreType.DMA
    pieces = pl.pallas_call(
        kernel,
        out_shape=jax.ShapeDtypeStruct((NO, 2, 16, T), BF16),
        in_specs=[hbm] * 8,
        out_specs=hbm,
        scratch_shapes=[
            pltpu.VMEM((1, NO, 8, 2 * T), BF16),
            pltpu.VMEM((1, NO, 8, 2 * T), F32),
            pltpu.SMEM((1, NO), I32),
            pltpu.SMEM((1, 2, NO), I32),
            pltpu.SMEM((1, NO), I32),
            pltpu.SMEM((NO,), F32),
            pltpu.VMEM((1, T), BF16),
            pltpu.VMEM((NO, 2, 16, T), BF16),
            pltpu.VMEM((2, NV, 16, T), BF16),
            pltpu.VMEM((NV, 16, T), BF16),
            pltpu.VMEM((NV, 2, 16, T), BF16),
            pltpu.VMEM((2, NV, 16, T), BF16),
            pltpu.VMEM((1, T), F32),
            pltpu.VMEM((NV, 1, T), F32),
            pltpu.VMEM((1, T), I32),
            pltpu.VMEM((NO, 1, T), I32),
            pltpu.SMEM((NO, 1, T), I32),
            pltpu.SMEM((2 * NV,), I32),
            pltpu.VMEM((3, 2, T, T), F32),
            pltpu.VMEM((3, 2, T, T), F32),
            pltpu.VMEM((3, T, T), F32),
            pltpu.VMEM((3, T, T), F32),
            pltpu.VMEM((2, NV, 16, T), BF16),
        ]
        + [sem] * 13
        + [sem((7,)), pltpu.SemaphoreType.REGULAR, pltpu.SemaphoreType.REGULAR],
        compiler_params=pltpu.CompilerParams(
            collective_id=0, has_side_effects=True, vmem_limit_bytes=64 << 20
        ),
    )(lam, drive, order, jnp.swapaxes(dom_tiles, 1, 2), dom_len, factors.reshape(1, 4 * T, T), e_occ, e_virt)
    return pl.pallas_call(
        unpack,
        out_shape=(
            jax.ShapeDtypeStruct((1, NO, 8, 2 * T), BF16),
            jax.ShapeDtypeStruct((2, 1, NO), F32),
        ),
        in_specs=[vmem, smem, smem],
        out_specs=(vmem, vmem),
        compiler_params=pltpu.CompilerParams(vmem_limit_bytes=64 << 20),
    )(pieces, order, dom_len)


def solution(mesh):
    return jax.shard_map(
        shards,
        mesh=mesh,
        in_specs=(
            P("pair", None, "virt", None),
            P("pair", None, "virt", None),
            P("pair", None),
            P("pair", None, None),
            P("pair", None),
            P("virt", None, None, None),
            P(),
            P("virt", None),
        ),
        out_specs=(P("pair", None, "virt", None), P(None, "pair", None)),
        check_vma=False,
    )
```

```python
import functools

import jax
import jax.numpy as jnp
from jax import lax
from jax.experimental import pallas as pl
from jax.experimental.pallas import tpu as pltpu
from jax.sharding import PartitionSpec as P

F32, BF16, I32 = jnp.float32, jnp.bfloat16, jnp.int32
MESH = pl.DeviceIdType.MESH
NZ, NV, NO, T = 8, 32, 16, 128
EARLY = 4
Y_ORDER = (4, 3, 5, 2, 6, 1, 7)


def host_of(i, j, ty):
    diag = i == j
    low, high = jnp.minimum(i, j), jnp.maximum(i, j)
    rank = lax.div(low * (31 - low), 2) + high - low - 1
    plane = jnp.where(diag, lax.div(i, 2), lax.div(rank, 15))
    virt = jnp.where(diag, lax.rem(i, 2), 2 + 2 * lax.rem(rank, 15) + ty)
    return plane, virt, jnp.where(diag, ty, (i > j).astype(I32))


def pair_of(plane, v):
    g = lax.div(v, 2)
    rank = 15 * plane + jnp.maximum(g - 1, 0)
    low = sum((rank >= n * (31 - n) // 2).astype(I32) for n in range(1, 15))
    high = rank - lax.div(low * (31 - low), 2) + low + 1
    own = 2 * plane + lax.rem(v, 2)
    return jnp.where(g == 0, own, low), jnp.where(g == 0, own, high)


def kernel(
    lam_in, drive_in, order_in, tiles_in, lens_in, factors, e_occ_in, e_virt_in,
    orecv,
    lam, drive, order, tiles, lens, e_occ, e_virt,
    send, recv, buf1, sel, buf2, ev_own, evb, tab_own, tab, tab_s, pairs, cur, drv, den, inv, osend,
    s_amp, r_amp, s_fac, r_fac, s_ev, r_ev, s_tab, r_tab, s_sel, r_sel, s_out, r_out, l_sem, in_sems, column, ready,
):
    p, v = lax.axis_index("pair"), lax.axis_index("virt")
    z, c = lax.div(p, 2), lax.rem(p, 2)
    x, y = lax.div(v, 8), lax.rem(v, 8)
    k_own = lax.div(v, 16)
    host = c == 1
    my_i, my_j = pair_of(z, v)
    my_t = lax.rem(v, 2)
    diag = lax.div(v, 2) == 0
    row_1 = jnp.where(diag, my_i, my_j)
    early = z < EARLY

    def remote(src, dst, ss, rs, pp, vv):
        return pltpu.make_async_remote_copy(
            src_ref=src, dst_ref=dst, send_sem=ss, recv_sem=rs,
            device_id={"pair": pp, "virt": vv}, device_id_type=MESH,
        )

    def drain(ref, sem):
        pltpu.make_async_copy(ref, ref, sem).wait()

    loads = [
        pltpu.make_async_copy(src, dst, in_sems.at[n])
        for n, (src, dst) in enumerate([
            (tiles_in, tiles), (lens_in, lens), (order_in, order), (lam_in, lam), (drive_in, drive),
            (e_virt_in, e_virt), (e_occ_in, e_occ),
        ])
    ]
    tab[...] = jnp.zeros_like(tab)

    barrier = pltpu.get_barrier_semaphore()

    def greet(pp, vv):
        pl.semaphore_signal(barrier, inc=1, device_id={"pair": pp, "virt": vv}, device_id_type=MESH)

    def at_z(dz):
        return 2 * lax.rem(z + dz, NZ) + 1

    at_x = [8 * lax.rem(x + dx, 4) for dx in range(4)]
    at_y = [lax.rem(y + dy, 8) for dy in range(8)]
    places = [at_x[dx] + at_y[dy] for dy in Y_ORDER + (0,) for dx in (2, 1, 3, 0)][:-1]

    @pl.when(host)
    def _():
        for place in places:
            greet(p, place)
        for dz in Y_ORDER:
            greet(at_z(dz) - 1, v)
        greet(p - 1, v)

        @pl.when(early)
        def _():
            @pl.loop(0, NV)
            def _(w):
                for row in (my_i, row_1):
                    greet(2 * lax.div(row, 2), w)

    for load in loads:
        load.start()

    targets = []
    for j in range(NO):
        for h in range(2):
            zh, vh, side = host_of(p, j, lax.rem(k_own + h, 2))
            own = jnp.logical_and(2 * zh + 1 == p, vh == v)
            targets.append((j, h, 2 * zh + 1, vh, side, own, zh < EARLY))
    greetings = NZ
    for j in range(NO):
        for row in range(2):
            greetings += 2 * (host_of(2 * z + row, j, 0)[0] < EARLY).astype(I32)

    def away(own, act):
        pl.when(jnp.logical_not(own))(act)

    @pl.when(host)
    def _():
        @pl.loop(0, NV)
        def _(w):
            i, j = pair_of(z, w)
            pairs[2 * w] = i
            pairs[2 * w + 1] = 2 * j

    for load in loads[:2]:
        load.wait()
    lane = lax.broadcasted_iota(I32, (1, T), 1)
    row_table = jnp.zeros((1, T), I32)
    for j in range(NO):
        for k in range(2):
            row_table = jnp.where(lane == 2 * j + k, tiles[0, k, j], row_table)
        row_table = jnp.where(lane == 32 + j, lens[0, j], row_table)
    tab_own[...] = row_table

    def slice_at(place):
        return factors.at[0, pl.ds(pl.multiple_of(16 * place, 16), 16)]

    def slice_copy(place):
        return remote(slice_at(place), buf1.at[v], s_fac, r_fac, p, place)

    def ev_copy(place):
        return remote(ev_own, evb.at[v], s_ev, r_ev, p, place)

    def tab_copy(dz):
        return remote(tab_own, tab.at[p], s_tab, r_tab, at_z(dz), v)

    def near_tables(dz, act):
        pl.when(z + dz < NZ)(lambda: act(tab_copy(dz)))

    def send_tables(first):
        for dz in range(first, 4):
            near_tables(dz, lambda copy: copy.start())

    def tell(sem, pp):
        pl.semaphore_signal(sem, inc=1, device_id={"pair": pp, "virt": v}, device_id_type=MESH)

    for load in loads[2:]:
        load.wait()
    ev_own[...] = e_virt[...].astype(F32)

    def find(s, found):
        o = order[0, s]
        return tuple(
            jnp.where(o == n, s, f) for n, f in enumerate(found)
        )

    slots = lax.fori_loop(0, NO, find, (jnp.int32(0),) * NO)
    for n in range(NO):
        own_lam = lam[0, slots[n]].astype(F32)
        own_drive = drive[0, slots[n]]
        for h in range(2):
            cols = slice(h * T, (h + 1) * T)
            send[n, h] = jnp.concatenate([own_lam[:, cols], own_drive[:, cols]], axis=0).astype(BF16)

    def amp_copy(n, h, side, pp, vv):
        return remote(send.at[n, h], recv.at[side, v], s_amp, r_amp, pp, vv)

    def send_amplitudes(to_early):
        for n, h, pp, vv, side, own, at_early in targets:
            now = at_early if to_early else jnp.logical_not(at_early)

            @pl.when(jnp.logical_and(now, jnp.logical_not(own)))
            def _():
                amp_copy(n, h, side, pp, vv).start()

            @pl.when(jnp.logical_and(now, own))
            def _():
                pltpu.make_async_copy(send.at[n, h], recv.at[side, v], r_amp).start()

    @pl.when(host)
    def _():
        pl.semaphore_wait(barrier, NV - 1)

        for place in places:
            slice_copy(place).start()
        for place in places:
            ev_copy(place).start()
        pltpu.make_async_copy(slice_at(v), buf1.at[v], r_fac).start()
        pltpu.make_async_copy(ev_own, evb.at[v], r_ev).start()
        pltpu.make_async_copy(tab_own, tab.at[p], r_tab).start()

    @pl.when(jnp.logical_not(host))
    def _():
        pl.semaphore_wait(barrier, greetings)
        tell(column, p + 1)
        send_tables(0)
        send_amplitudes(True)

    def tile(w, k):
        return tab_s[pairs[2 * w], 0, pairs[2 * w + 1] + k]

    def send_slices():
        drain(buf1, r_fac)
        for w in places:
            for k in range(2):
                sel[w, k] = buf1[tile(w, k)]
            remote(sel.at[w], buf2.at[:, v], s_sel, r_sel, p, w).start()
        for k in range(2):
            sel[v, k] = buf1[tile(v, k)]
        pltpu.make_async_copy(sel.at[v], buf2.at[:, v], r_sel).start()

    @pl.when(host)
    def _():
        pl.semaphore_wait(column, 1)
        for dz in Y_ORDER:
            tell(ready, at_z(dz))
        send_tables(1)
        send_amplitudes(True)
        for n in range(1, 5):
            @pl.when(jnp.minimum(z, 3) + 1 == n)
            def _():
                drain(tab.at[0 : 2 * n], r_tab)
        to_smem = pltpu.make_async_copy(tab, tab_s, l_sem)
        to_smem.start()
        to_smem.wait()
        pl.when(z < 2)(send_slices)
        pl.semaphore_wait(ready, NZ - 1)
        tell(ready, p - 1)

    @pl.when(jnp.logical_not(host))
    def _():
        pl.semaphore_wait(ready, 1)

    send_amplitudes(False)

    @pl.when(host)
    def _():
        pl.when(z >= 2)(send_slices)
        own_tiles = [tile(v, k) for k in range(2)]
        length = tab_s[my_i, 0, 32 + my_j]
        occ = e_occ[my_i] + e_occ[my_j]
        drain(evb, r_ev)
        e_row = [evb[tile] for tile in own_tiles]
        e_col = [jnp.transpose(jnp.broadcast_to(e, (T, T))) for e in e_row]

        crossed = jnp.logical_and(jnp.logical_not(diag), my_t == 1)
        couples = [
            (0, 0, jnp.where(diag, 0, 1), jnp.where(crossed, 1, 0)),
            (0, 1, jnp.where(diag, 0, 1), jnp.where(crossed, 0, 1)),
            (1, 0, 1, 1),
        ]

        def alive(pk, l):
            return jnp.logical_and(pk < length, l < length)

        def divide(o):
            ps, pk, qs, l = couples[o]
            e_l = jnp.where(l == 0, e_row[0], e_row[1])
            gap = e_col[pk] + e_l - occ
            den[o] = gap
            inv[o] = 1.0 / gap

        def prepare(o):
            ps, pk, qs, l = couples[o]
            first = recv[ps, pl.ds(16 * pk, 16)].astype(F32).reshape(16, 2, 8, T)
            second = recv[qs, pl.ds(16 * l, 16)].astype(F32).reshape(16, 2, 8, T)
            live = alive(pk, l)
            cur[o, 0] = jnp.where(live, first[:, 0].reshape(T, T), 0.0)
            cur[o, 1] = jnp.where(live, jnp.transpose(second[:, 0].reshape(T, T)), 0.0)
            drv[o, 0] = first[:, 1].reshape(T, T)
            drv[o, 1] = jnp.transpose(second[:, 1].reshape(T, T))

        def iterate(o):
            ps, pk, qs, l = couples[o]
            right = buf2[l].reshape(4 * T, T)
            left = buf2[pk].reshape(4 * T, T)
            live = alive(pk, l)
            now = [cur[o, 0], cur[o, 1]]
            squares = []
            for it in range(2):
                half = lax.dot_general(
                    (now[0] + now[1]).astype(BF16), right, (((1,), (1,)), ((), ())),
                    preferred_element_type=F32,
                ).astype(BF16)
                ladder = jnp.zeros((T, T), F32)
                for q in range(4):
                    rows = slice(q * T, (q + 1) * T)
                    ladder += jnp.dot(left[rows], half[:, rows], preferred_element_type=F32)
                ladder = ladder.astype(BF16).astype(F32)
                for n in range(2):
                    target = drv[o, n] + ladder
                    resid = jnp.where(live, target - den[o] * now[n], 0.0)
                    now[n] = jnp.where(live, target * inv[o], 0.0).astype(BF16).astype(F32)
                    squares.append(jnp.sum(resid * resid, axis=0, keepdims=True))
            return now[0], jnp.transpose(now[1]), squares

        def norm_rows(first, second):
            rows = jnp.zeros((8, T), F32)
            sub = lax.broadcasted_iota(I32, (8, T), 0)
            for it, total in enumerate((first, second)):
                total = jnp.broadcast_to(jnp.sum(total, axis=1, keepdims=True), (8, T))
                high = total.astype(BF16).astype(F32)
                rows = jnp.where(sub == 2 * it, high, jnp.where(sub == 2 * it + 1, total - high, rows))
            return jnp.broadcast_to(rows[None], (16, 8, T))

        def post(side, block, values, rows):
            message = jnp.concatenate([values.reshape(16, 8, T), rows], axis=1)
            osend[side, pl.ds(16 * block, 16)] = message.astype(BF16)

        for o in range(3):
            divide(o)
        drain(recv, r_amp)
        for o in range(2):
            prepare(o)
        pl.when(diag)(lambda: prepare(2))
        drain(buf2, r_sel)
        done = [iterate(o) for o in range(2)]
        sums = [done[0][2][n] + done[1][2][n] for n in range(4)]
        rows = norm_rows(sums[0], sums[2])
        for o in range(2):
            post(0, o, done[o][0], rows)

        @pl.when(jnp.logical_not(diag))
        def _():
            rows = norm_rows(sums[1], sums[3])
            for o in range(2):
                post(1, couples[o][3], done[o][1], rows)

        @pl.when(diag)
        def _():
            first, second, squares = iterate(2)
            rows = norm_rows(squares[0] + squares[1], squares[2] + squares[3])
            post(1, 0, first, rows)
            post(1, 1, second, rows)

        for s in range(2):
            row, col = (my_i, my_j) if s == 0 else (row_1, my_i)

            @pl.loop(0, NV)
            def _(w):
                half = lax.rem(lax.div(w, 16) + jnp.where(diag, s, my_t), 2)
                dst = orecv.at[col, half]
                self_home = jnp.logical_and(row == p, w == v)

                @pl.when(jnp.logical_not(self_home))
                def _():
                    remote(osend.at[s, w], dst, s_out, r_out, row, w).start()

                @pl.when(self_home)
                def _():
                    pltpu.make_async_copy(osend.at[s, w], dst, r_out).start()

    for n, h, pp, vv, side, own, _ in targets:
        away(own, lambda: amp_copy(n, h, side, pp, vv).wait_send())
    for dz in range(1, 4):
        near_tables(dz, lambda copy: copy.wait_send())

    @pl.when(jnp.logical_not(host))
    def _():
        tab_copy(0).wait_send()

    @pl.when(host)
    def _():
        drain(buf1.at[0 : NV - 1], s_fac)
        drain(evb.at[0 : NV - 1], s_ev)
        drain(sel.at[0 : NV - 1], s_sel)
        for s in range(2):
            row = my_i if s == 0 else row_1

            @pl.loop(0, NV)
            def _(w):
                @pl.when(jnp.logical_not(jnp.logical_and(row == p, w == v)))
                def _():
                    remote(osend.at[s, w], osend.at[s, w], s_out, r_out, row, w).wait_send()

    drain(orecv, r_out)


def unpack(orecv, order, lens, out, norms):
    lane = lax.broadcasted_iota(I32, (1, T), 1)
    totals = [jnp.zeros((1, T), F32), jnp.zeros((1, T), F32)]
    count = jnp.ones((1, T), F32)
    for s in range(NO):
        j = order[0, s]
        pieces = [orecv[j, h].astype(F32) for h in range(2)]
        out[0, s] = jnp.concatenate([piece[:8] for piece in pieces], axis=1).astype(BF16)
        both = pieces[0][8:] + pieces[1][8:]
        totals = [
            jnp.where(lane == s, both[2 * it : 2 * it + 1] + both[2 * it + 1 : 2 * it + 2], totals[it])
            for it in range(2)
        ]
        size = (lens[0, j] * T).astype(F32)
        count = jnp.where(lane == s, size * size, count)
    for it in range(2):
        norms[it] = jnp.sqrt(totals[it] / count + 1e-6)[:, :NO]


def shards(lam, drive, order, dom_tiles, dom_len, factors, e_occ, e_virt):
    vmem, smem = pl.BlockSpec(memory_space=pltpu.VMEM), pl.BlockSpec(memory_space=pltpu.SMEM)
    hbm = pl.BlockSpec(memory_space=pltpu.HBM)
    sem = pltpu.SemaphoreType.DMA
    pieces = pl.pallas_call(
        kernel,
        out_shape=jax.ShapeDtypeStruct((NO, 2, 16, T), BF16),
        in_specs=[hbm] * 8,
        out_specs=hbm,
        scratch_shapes=[
            pltpu.VMEM((1, NO, 8, 2 * T), BF16),
            pltpu.VMEM((1, NO, 8, 2 * T), F32),
            pltpu.SMEM((1, NO), I32),
            pltpu.SMEM((1, 2, NO), I32),
            pltpu.SMEM((1, NO), I32),
            pltpu.SMEM((NO,), F32),
            pltpu.VMEM((1, T), BF16),
            pltpu.VMEM((NO, 2, 16, T), BF16),
            pltpu.VMEM((2, NV, 16, T), BF16),
            pltpu.VMEM((NV, 16, T), BF16),
            pltpu.VMEM((NV, 2, 16, T), BF16),
            pltpu.VMEM((2, NV, 16, T), BF16),
            pltpu.VMEM((1, T), F32),
            pltpu.VMEM((NV, 1, T), F32),
            pltpu.VMEM((1, T), I32),
            pltpu.VMEM((NO, 1, T), I32),
            pltpu.SMEM((NO, 1, T), I32),
            pltpu.SMEM((2 * NV,), I32),
            pltpu.VMEM((3, 2, T, T), F32),
            pltpu.VMEM((3, 2, T, T), F32),
            pltpu.VMEM((3, T, T), F32),
            pltpu.VMEM((3, T, T), F32),
            pltpu.VMEM((2, NV, 16, T), BF16),
        ]
        + [sem] * 13
        + [sem((7,)), pltpu.SemaphoreType.REGULAR, pltpu.SemaphoreType.REGULAR],
        compiler_params=pltpu.CompilerParams(
            collective_id=0, has_side_effects=True, vmem_limit_bytes=64 << 20
        ),
    )(lam, drive, order, jnp.swapaxes(dom_tiles, 1, 2), dom_len, factors.reshape(1, 4 * T, T), e_occ, e_virt)
    return pl.pallas_call(
        unpack,
        out_shape=(
            jax.ShapeDtypeStruct((1, NO, 8, 2 * T), BF16),
            jax.ShapeDtypeStruct((2, 1, NO), F32),
        ),
        in_specs=[vmem, smem, smem],
        out_specs=(vmem, vmem),
        compiler_params=pltpu.CompilerParams(vmem_limit_bytes=64 << 20),
    )(pieces, order, dom_len)


def solution(mesh):
    return jax.shard_map(
        shards,
        mesh=mesh,
        in_specs=(
            P("pair", None, "virt", None),
            P("pair", None, "virt", None),
            P("pair", None),
            P("pair", None, None),
            P("pair", None),
            P("virt", None, None, None),
            P(),
            P("virt", None),
        ),
        out_specs=(P("pair", None, "virt", None), P(None, "pair", None)),
        check_vma=False,
    )
```

```python
import functools

import jax
import jax.numpy as jnp
from jax import lax
from jax.experimental import pallas as pl
from jax.experimental.pallas import tpu as pltpu
from jax.sharding import PartitionSpec as P

F32, BF16, I32 = jnp.float32, jnp.bfloat16, jnp.int32
MESH = pl.DeviceIdType.MESH
NZ, NV, NO, T = 8, 32, 16, 128
EARLY = 4
Y_ORDER = (4, 3, 5, 2, 6, 1, 7)


def host_of(i, j, ty):
    diag = i == j
    low, high = jnp.minimum(i, j), jnp.maximum(i, j)
    rank = lax.div(low * (31 - low), 2) + high - low - 1
    plane = jnp.where(diag, lax.div(i, 2), lax.div(rank, 15))
    virt = jnp.where(diag, lax.rem(i, 2), 2 + 2 * lax.rem(rank, 15) + ty)
    return plane, virt, jnp.where(diag, ty, (i > j).astype(I32))


def pair_of(plane, v):
    g = lax.div(v, 2)
    rank = 15 * plane + jnp.maximum(g - 1, 0)
    low = sum((rank >= n * (31 - n) // 2).astype(I32) for n in range(1, 15))
    high = rank - lax.div(low * (31 - low), 2) + low + 1
    own = 2 * plane + lax.rem(v, 2)
    return jnp.where(g == 0, own, low), jnp.where(g == 0, own, high)


def kernel(
    lam_in, drive_in, order_in, tiles_in, lens_in, factors, e_occ_in, e_virt_in,
    orecv,
    lam, drive, order, tiles, lens, e_occ, e_virt,
    send, recv, buf1, sel, buf2, ev_own, evb, tab_own, tab, tab_s, pairs, cur, drv, den, inv, osend,
    s_amp, r_amp, s_fac, r_fac, s_ev, r_ev, s_tab, r_tab, s_sel, r_sel, s_out, r_out, l_sem, in_sems, column, ready,
):
    p, v = lax.axis_index("pair"), lax.axis_index("virt")
    z, c = lax.div(p, 2), lax.rem(p, 2)
    x, y = lax.div(v, 8), lax.rem(v, 8)
    k_own = lax.div(v, 16)
    host = c == 1
    my_i, my_j = pair_of(z, v)
    my_t = lax.rem(v, 2)
    diag = lax.div(v, 2) == 0
    row_1 = jnp.where(diag, my_i, my_j)
    early = z < EARLY

    def remote(src, dst, ss, rs, pp, vv):
        return pltpu.make_async_remote_copy(
            src_ref=src, dst_ref=dst, send_sem=ss, recv_sem=rs,
            device_id={"pair": pp, "virt": vv}, device_id_type=MESH,
        )

    def drain(ref, sem):
        pltpu.make_async_copy(ref, ref, sem).wait()

    loads = [
        pltpu.make_async_copy(src, dst, in_sems.at[n])
        for n, (src, dst) in enumerate([
            (tiles_in, tiles), (lens_in, lens), (order_in, order), (lam_in, lam), (drive_in, drive),
            (e_virt_in, e_virt), (e_occ_in, e_occ),
        ])
    ]
    tab[...] = jnp.zeros_like(tab)

    barrier = pltpu.get_barrier_semaphore()

    def greet(pp, vv):
        pl.semaphore_signal(barrier, inc=1, device_id={"pair": pp, "virt": vv}, device_id_type=MESH)

    def at_z(dz):
        return 2 * lax.rem(z + dz, NZ) + 1

    at_x = [8 * lax.rem(x + dx, 4) for dx in range(4)]
    at_y = [lax.rem(y + dy, 8) for dy in range(8)]
    places = [at_x[dx] + at_y[dy] for dy in Y_ORDER + (0,) for dx in (2, 1, 3, 0)][:-1]

    @pl.when(host)
    def _():
        for place in places:
            greet(p, place)
        for dz in Y_ORDER:
            greet(at_z(dz) - 1, v)
        greet(p - 1, v)

        @pl.when(early)
        def _():
            @pl.loop(0, NV)
            def _(w):
                for row in (my_i, row_1):
                    greet(2 * lax.div(row, 2), w)

    for load in loads:
        load.start()

    targets = []
    for j in range(NO):
        for h in range(2):
            zh, vh, side = host_of(p, j, lax.rem(k_own + h, 2))
            own = jnp.logical_and(2 * zh + 1 == p, vh == v)
            targets.append((j, h, 2 * zh + 1, vh, side, own, zh < EARLY))
    greetings = NZ
    for j in range(NO):
        for row in range(2):
            greetings += 2 * (host_of(2 * z + row, j, 0)[0] < EARLY).astype(I32)

    def away(own, act):
        pl.when(jnp.logical_not(own))(act)

    @pl.when(host)
    def _():
        @pl.loop(0, NV)
        def _(w):
            i, j = pair_of(z, w)
            pairs[2 * w] = i
            pairs[2 * w + 1] = 2 * j

    for load in loads[:2]:
        load.wait()
    lane = lax.broadcasted_iota(I32, (1, T), 1)
    row_table = jnp.zeros((1, T), I32)
    for j in range(NO):
        for k in range(2):
            row_table = jnp.where(lane == 2 * j + k, tiles[0, k, j], row_table)
        row_table = jnp.where(lane == 32 + j, lens[0, j], row_table)
    tab_own[...] = row_table

    def slice_at(place):
        return factors.at[0, pl.ds(pl.multiple_of(16 * place, 16), 16)]

    def slice_copy(place):
        return remote(slice_at(place), buf1.at[v], s_fac, r_fac, p, place)

    def ev_copy(place):
        return remote(ev_own, evb.at[v], s_ev, r_ev, p, place)

    def tab_copy(dz):
        return remote(tab_own, tab.at[p], s_tab, r_tab, at_z(dz), v)

    def near_tables(dz, act):
        pl.when(z + dz < NZ)(lambda: act(tab_copy(dz)))

    def send_tables(first):
        for dz in range(first, 4):
            near_tables(dz, lambda copy: copy.start())

    def tell(sem, pp):
        pl.semaphore_signal(sem, inc=1, device_id={"pair": pp, "virt": v}, device_id_type=MESH)

    for load in loads[2:]:
        load.wait()
    ev_own[...] = e_virt[...].astype(F32)

    def find(s, found):
        o = order[0, s]
        return tuple(
            jnp.where(o == n, s, f) for n, f in enumerate(found)
        )

    slots = lax.fori_loop(0, NO, find, (jnp.int32(0),) * NO)
    for n in range(NO):
        own_lam = lam[0, slots[n]].astype(F32)
        own_drive = drive[0, slots[n]]
        for h in range(2):
            cols = slice(h * T, (h + 1) * T)
            send[n, h] = jnp.concatenate([own_lam[:, cols], own_drive[:, cols]], axis=0).astype(BF16)

    def amp_copy(n, h, side, pp, vv):
        return remote(send.at[n, h], recv.at[side, v], s_amp, r_amp, pp, vv)

    def send_amplitudes(to_early):
        for n, h, pp, vv, side, own, at_early in targets:
            now = at_early if to_early else jnp.logical_not(at_early)

            @pl.when(jnp.logical_and(now, jnp.logical_not(own)))
            def _():
                amp_copy(n, h, side, pp, vv).start()

            @pl.when(jnp.logical_and(now, own))
            def _():
                pltpu.make_async_copy(send.at[n, h], recv.at[side, v], r_amp).start()

    @pl.when(host)
    def _():
        pl.semaphore_wait(barrier, NV - 1)

        for place in places:
            slice_copy(place).start()
        for place in places:
            ev_copy(place).start()
        pltpu.make_async_copy(slice_at(v), buf1.at[v], r_fac).start()
        pltpu.make_async_copy(ev_own, evb.at[v], r_ev).start()
        pltpu.make_async_copy(tab_own, tab.at[p], r_tab).start()

    @pl.when(jnp.logical_not(host))
    def _():
        pl.semaphore_wait(barrier, greetings)
        tell(column, p + 1)
        send_tables(0)
        send_amplitudes(True)

    def tile(w, k):
        return tab_s[pairs[2 * w], 0, pairs[2 * w + 1] + k]

    def send_slices():
        drain(buf1, r_fac)
        for w in places:
            for k in range(2):
                sel[w, k] = buf1[tile(w, k)]
            remote(sel.at[w], buf2.at[:, v], s_sel, r_sel, p, w).start()
        for k in range(2):
            sel[v, k] = buf1[tile(v, k)]
        pltpu.make_async_copy(sel.at[v], buf2.at[:, v], r_sel).start()

    @pl.when(host)
    def _():
        pl.semaphore_wait(column, 1)
        for dz in Y_ORDER:
            tell(ready, at_z(dz))
        send_tables(1)
        send_amplitudes(True)
        for n in range(1, 5):
            @pl.when(jnp.minimum(z, 3) + 1 == n)
            def _():
                drain(tab.at[0 : 2 * n], r_tab)
        to_smem = pltpu.make_async_copy(tab, tab_s, l_sem)
        to_smem.start()
        to_smem.wait()
        pl.when(z < 2)(send_slices)
        pl.semaphore_wait(ready, NZ - 1)
        tell(ready, p - 1)

    @pl.when(jnp.logical_not(host))
    def _():
        pl.semaphore_wait(ready, 1)

    send_amplitudes(False)

    @pl.when(host)
    def _():
        pl.when(z >= 2)(send_slices)
        own_tiles = [tile(v, k) for k in range(2)]
        length = tab_s[my_i, 0, 32 + my_j]
        occ = e_occ[my_i] + e_occ[my_j]
        drain(evb, r_ev)
        e_row = [evb[tile] for tile in own_tiles]
        e_col = [jnp.transpose(jnp.broadcast_to(e, (T, T))) for e in e_row]

        crossed = jnp.logical_and(jnp.logical_not(diag), my_t == 1)
        couples = [
            (0, 0, jnp.where(diag, 0, 1), jnp.where(crossed, 1, 0)),
            (0, 1, jnp.where(diag, 0, 1), jnp.where(crossed, 0, 1)),
            (1, 0, 1, 1),
        ]

        def alive(pk, l):
            return jnp.logical_and(pk < length, l < length)

        def divide(o):
            ps, pk, qs, l = couples[o]
            e_l = jnp.where(l == 0, e_row[0], e_row[1])
            gap = e_col[pk] + e_l - occ
            den[o] = gap
            inv[o] = 1.0 / gap

        def prepare(o):
            ps, pk, qs, l = couples[o]
            first = recv[ps, pl.ds(16 * pk, 16)].astype(F32).reshape(16, 2, 8, T)
            second = recv[qs, pl.ds(16 * l, 16)].astype(F32).reshape(16, 2, 8, T)
            live = alive(pk, l)
            cur[o, 0] = jnp.where(live, first[:, 0].reshape(T, T), 0.0)
            cur[o, 1] = jnp.where(live, jnp.transpose(second[:, 0].reshape(T, T)), 0.0)
            drv[o, 0] = first[:, 1].reshape(T, T)
            drv[o, 1] = jnp.transpose(second[:, 1].reshape(T, T))

        def iterate(o):
            ps, pk, qs, l = couples[o]
            right = buf2[l].reshape(4 * T, T)
            left = buf2[pk].reshape(4 * T, T)
            live = alive(pk, l)
            now = [cur[o, 0], cur[o, 1]]
            squares = []
            for it in range(2):
                half = lax.dot_general(
                    (now[0] + now[1]).astype(BF16), right, (((1,), (1,)), ((), ())),
                    preferred_element_type=F32,
                ).astype(BF16)
                ladder = jnp.zeros((T, T), F32)
                for q in range(4):
                    rows = slice(q * T, (q + 1) * T)
                    ladder += jnp.dot(left[rows], half[:, rows], preferred_element_type=F32)
                ladder = ladder.astype(BF16).astype(F32)
                for n in range(2):
                    target = drv[o, n] + ladder
                    resid = jnp.where(live, target - den[o] * now[n], 0.0)
                    now[n] = jnp.where(live, target * inv[o], 0.0).astype(BF16).astype(F32)
                    squares.append(jnp.sum(resid * resid, axis=0, keepdims=True))
            return now[0], jnp.transpose(now[1]), squares

        def norm_rows(first, second):
            rows = jnp.zeros((8, T), F32)
            sub = lax.broadcasted_iota(I32, (8, T), 0)
            for it, total in enumerate((first, second)):
                total = jnp.broadcast_to(jnp.sum(total, axis=1, keepdims=True), (8, T))
                high = total.astype(BF16).astype(F32)
                rows = jnp.where(sub == 2 * it, high, jnp.where(sub == 2 * it + 1, total - high, rows))
            return jnp.broadcast_to(rows[None], (16, 8, T))

        def post(side, block, values, rows):
            message = jnp.concatenate([values.reshape(16, 8, T), rows], axis=1)
            osend[side, pl.ds(16 * block, 16)] = message.astype(BF16)

        for o in range(3):
            divide(o)
        drain(recv, r_amp)
        for o in range(2):
            prepare(o)
        pl.when(diag)(lambda: prepare(2))
        drain(buf2, r_sel)
        done = [iterate(o) for o in range(2)]
        sums = [done[0][2][n] + done[1][2][n] for n in range(4)]
        rows = norm_rows(sums[0], sums[2])
        for o in range(2):
            post(0, o, done[o][0], rows)

        @pl.when(jnp.logical_not(diag))
        def _():
            rows = norm_rows(sums[1], sums[3])
            for o in range(2):
                post(1, couples[o][3], done[o][1], rows)

        @pl.when(diag)
        def _():
            first, second, squares = iterate(2)
            rows = norm_rows(squares[0] + squares[1], squares[2] + squares[3])
            post(1, 0, first, rows)
            post(1, 1, second, rows)

        for s in range(2):
            row, col = (my_i, my_j) if s == 0 else (row_1, my_i)

            def landing(w):
                return orecv.at[col, lax.rem(lax.div(w, 16) + jnp.where(diag, s, my_t), 2)]

            for w in places:
                remote(osend.at[s, w], landing(w), s_out, r_out, row, w).start()

            @pl.when(row != p)
            def _():
                remote(osend.at[s, v], landing(v), s_out, r_out, row, v).start()

            @pl.when(row == p)
            def _():
                pltpu.make_async_copy(osend.at[s, v], landing(v), r_out).start()

    for n, h, pp, vv, side, own, _ in targets:
        away(own, lambda: amp_copy(n, h, side, pp, vv).wait_send())
    for dz in range(1, 4):
        near_tables(dz, lambda copy: copy.wait_send())

    @pl.when(jnp.logical_not(host))
    def _():
        tab_copy(0).wait_send()

    @pl.when(host)
    def _():
        drain(buf1.at[0 : NV - 1], s_fac)
        drain(evb.at[0 : NV - 1], s_ev)
        drain(sel.at[0 : NV - 1], s_sel)
        for s in range(2):
            row = my_i if s == 0 else row_1

            @pl.loop(0, NV)
            def _(w):
                @pl.when(jnp.logical_not(jnp.logical_and(row == p, w == v)))
                def _():
                    remote(osend.at[s, w], osend.at[s, w], s_out, r_out, row, w).wait_send()

    drain(orecv, r_out)


def unpack(orecv, order, lens, out, norms):
    lane = lax.broadcasted_iota(I32, (1, T), 1)
    totals = [jnp.zeros((1, T), F32), jnp.zeros((1, T), F32)]
    count = jnp.ones((1, T), F32)
    for s in range(NO):
        j = order[0, s]
        pieces = [orecv[j, h].astype(F32) for h in range(2)]
        out[0, s] = jnp.concatenate([piece[:8] for piece in pieces], axis=1).astype(BF16)
        both = pieces[0][8:] + pieces[1][8:]
        totals = [
            jnp.where(lane == s, both[2 * it : 2 * it + 1] + both[2 * it + 1 : 2 * it + 2], totals[it])
            for it in range(2)
        ]
        size = (lens[0, j] * T).astype(F32)
        count = jnp.where(lane == s, size * size, count)
    for it in range(2):
        norms[it] = jnp.sqrt(totals[it] / count + 1e-6)[:, :NO]


def shards(lam, drive, order, dom_tiles, dom_len, factors, e_occ, e_virt):
    vmem, smem = pl.BlockSpec(memory_space=pltpu.VMEM), pl.BlockSpec(memory_space=pltpu.SMEM)
    hbm = pl.BlockSpec(memory_space=pltpu.HBM)
    sem = pltpu.SemaphoreType.DMA
    pieces = pl.pallas_call(
        kernel,
        out_shape=jax.ShapeDtypeStruct((NO, 2, 16, T), BF16),
        in_specs=[hbm] * 8,
        out_specs=hbm,
        scratch_shapes=[
            pltpu.VMEM((1, NO, 8, 2 * T), BF16),
            pltpu.VMEM((1, NO, 8, 2 * T), F32),
            pltpu.SMEM((1, NO), I32),
            pltpu.SMEM((1, 2, NO), I32),
            pltpu.SMEM((1, NO), I32),
            pltpu.SMEM((NO,), F32),
            pltpu.VMEM((1, T), BF16),
            pltpu.VMEM((NO, 2, 16, T), BF16),
            pltpu.VMEM((2, NV, 16, T), BF16),
            pltpu.VMEM((NV, 16, T), BF16),
            pltpu.VMEM((NV, 2, 16, T), BF16),
            pltpu.VMEM((2, NV, 16, T), BF16),
            pltpu.VMEM((1, T), F32),
            pltpu.VMEM((NV, 1, T), F32),
            pltpu.VMEM((1, T), I32),
            pltpu.VMEM((NO, 1, T), I32),
            pltpu.SMEM((NO, 1, T), I32),
            pltpu.SMEM((2 * NV,), I32),
            pltpu.VMEM((3, 2, T, T), F32),
            pltpu.VMEM((3, 2, T, T), F32),
            pltpu.VMEM((3, T, T), F32),
            pltpu.VMEM((3, T, T), F32),
            pltpu.VMEM((2, NV, 16, T), BF16),
        ]
        + [sem] * 13
        + [sem((7,)), pltpu.SemaphoreType.REGULAR, pltpu.SemaphoreType.REGULAR],
        compiler_params=pltpu.CompilerParams(
            collective_id=0, has_side_effects=True, vmem_limit_bytes=64 << 20
        ),
    )(lam, drive, order, jnp.swapaxes(dom_tiles, 1, 2), dom_len, factors.reshape(1, 4 * T, T), e_occ, e_virt)
    return pl.pallas_call(
        unpack,
        out_shape=(
            jax.ShapeDtypeStruct((1, NO, 8, 2 * T), BF16),
            jax.ShapeDtypeStruct((2, 1, NO), F32),
        ),
        in_specs=[vmem, smem, smem],
        out_specs=(vmem, vmem),
        compiler_params=pltpu.CompilerParams(vmem_limit_bytes=64 << 20),
    )(pieces, order, dom_len)


def solution(mesh):
    return jax.shard_map(
        shards,
        mesh=mesh,
        in_specs=(
            P("pair", None, "virt", None),
            P("pair", None, "virt", None),
            P("pair", None),
            P("pair", None, None),
            P("pair", None),
            P("virt", None, None, None),
            P(),
            P("virt", None),
        ),
        out_specs=(P("pair", None, "virt", None), P(None, "pair", None)),
        check_vma=False,
    )
```
